256 devices in a mesh: dap: 128 (over x, z, y), dp: 2 (over core).
Axes of the slice: x: 4, y: 4, z: 8, core: 2. Of those that a mesh axis runs over, the one named last changes fastest.
Arguments:
- homolog_embedding_tensor: bfloat16 [64, 1024, 256], P('dp', 'dap'), parts along dimension 0, may hold values from -6 to 6
- standardizer_scale: float32 [256], replicated, may hold values from 0.1 to 1.9
- standardizer_shift: float32 [256], replicated, may hold values from -3 to 3
- first_operand_kernel: bfloat16 [256, 32], replicated, may hold values from -0.375 to 0.375
- left_projection_bias: float32 [32], replicated, may hold values from -3 to 3
- second_operand_kernel: bfloat16 [256, 32], replicated, may hold values from -0.375 to 0.375
- right_projection_bias: float32 [32], replicated, may hold values from -3 to 3
- output_weight_matrix: bfloat16 [1024, 128], replicated, may hold values from -0.75 to 0.75
- output_bias_vector: float32 [128], replicated, may hold values from -3 to 3
- pair_update_cotangent: bfloat16 [2048, 1024, 128], P(('dp', 'dap')), parts along dimension 0, may hold values from -24 to 24
Outputs:
- pair_representation_update: bfloat16 [2048, 1024, 128], P(('dp', 'dap')), parts along dimension 0
- alignment_gradient: float32 [64, 1024, 256], P('dp', 'dap'), parts along dimension 0
- norm_gain_gradient: float32 [512], P('dp'), parts along dimension 0
- norm_offset_gradient: float32 [512], P('dp'), parts along dimension 0
- left_weight_gradient: float32 [512, 32], P('dp'), parts along dimension 0
- left_bias_gradient: float32 [64], P('dp'), parts along dimension 0
- right_weight_gradient: float32 [512, 32], P('dp'), parts along dimension 0
- right_bias_gradient: float32 [64], P('dp'), parts along dimension 0
- output_weight_gradient: float32 [2048, 128], P('dp'), parts along dimension 0
- output_bias_gradient: float32 [256], P('dp'), parts along dimension 0
The draws below stay inside these ranges and needn't reach their ends.
There are 2 independent parts, one for each index of `dp`. The reference program is written for one: setup_inputs(seed, part) draws one part's arguments, and reference() takes and returns one part's arrays. A program takes and returns all parts, laid end to end along the dimension named above; an argument that names none is the same for every part. Nothing has to cross between parts.
All inputs are finite; a program needn't handle non-finite values.
Results may differ from the reference program's by a relative error of at most 0.0056.
Values may be sent and summed in bfloat16 or wider, within the bound.
No kernel may reach another device: no remote copies, remote signals or barrier semaphores. Data moves between devices by JAX's collectives and lax.ppermute only.
A program may use at most 128 MiB of HBM per device.

```python
import math
import jax
import jax.numpy as jnp
from jax import lax

FEATURE_DEPTH = 256
HIDDEN_WIDTH = 32
CZ = 128
HOMOLOG_TOTAL = 32
POSITION_TOTAL = 1024


def spiked(array, rng, source, target, blocks, factor):
    owner, partner = [(jnp.arange(array.shape[dim]) // (array.shape[dim] // blocks)).reshape([-1 if axis == dim else 1 for axis in range(array.ndim)]) for dim in (source, target)]
    chosen = jax.random.permutation(rng, blocks)[partner]
    strong = (owner == chosen) | (owner == (partner + blocks // 2) % blocks)
    return jnp.where(strong, factor * array, array)


def level_of(own_key, extent, split, least, high):
    def one(dim, blocks):
        steps = jax.random.uniform(jax.random.fold_in(jax.random.fold_in(own_key, 6), dim), (blocks,), jnp.float32, least / len(split), high / len(split))
        return jnp.repeat(jnp.exp(steps), extent[dim] // blocks).reshape((-1,) + (1,) * (len(extent) - dim - 1))

    loudness = one(*split[0])
    for cut in split[1:]:
        loudness = loudness * one(*cut)
    return loudness


def gaussian(own_key, shape, scale, reach, shards=(), kind=jnp.bfloat16):
    gain = level_of(own_key, shape, shards, -0.22, 0.18) if shards else 1.0
    array = jax.random.normal(own_key, shape, jnp.float32) * scale * gain
    return jnp.minimum(jnp.maximum(array, -reach), reach).astype(kind)


def noise_with(rng, shape, scale, reach, split, heavy, kind=jnp.bfloat16):
    entries = scale * jax.random.normal(rng, shape, jnp.float32)
    if split:
        entries = entries * level_of(rng, shape, split, -0.22, 0.18)
    return jnp.clip(spiked(entries, jax.random.fold_in(rng, 3), *heavy), -reach, reach).astype(kind)


def setup_inputs(seed: int = 0, part: int = 0) -> dict:
    seeds = jax.random.split(jax.random.key(seed), 11)
    part_splits = jax.random.split(jax.random.fold_in(seeds[10], part), 11)
    homolog_embedding_tensor = gaussian(part_splits[0], (HOMOLOG_TOTAL, POSITION_TOTAL, FEATURE_DEPTH), 1.0, 6.0, ((1, 128),))
    standardizer_scale = jnp.clip(1.0 + 0.18 * jax.random.normal(seeds[1], (FEATURE_DEPTH,), jnp.float32), 0.1, 1.9)
    standardizer_shift = gaussian(seeds[2], (FEATURE_DEPTH,), 0.5, 3.0, (), jnp.float32)
    first_operand_kernel = gaussian(seeds[3], (FEATURE_DEPTH, HIDDEN_WIDTH), FEATURE_DEPTH ** -0.5, 0.375)
    left_projection_bias = gaussian(seeds[4], (HIDDEN_WIDTH,), 0.5, 3.0, (), jnp.float32)
    second_operand_kernel = gaussian(seeds[5], (FEATURE_DEPTH, HIDDEN_WIDTH), FEATURE_DEPTH ** -0.5, 0.375)
    right_projection_bias = gaussian(seeds[6], (HIDDEN_WIDTH,), 0.5, 3.0, (), jnp.float32)
    output_weight_matrix = gaussian(seeds[7], (HIDDEN_WIDTH * HIDDEN_WIDTH, CZ), (HIDDEN_WIDTH * HIDDEN_WIDTH // 16) ** -0.5, 0.75)
    output_bias_vector = gaussian(seeds[8], (CZ,), 0.5, 3.0, (), jnp.float32)
    pair_update_cotangent = noise_with(part_splits[9], (POSITION_TOTAL, POSITION_TOTAL, CZ), 1.0, 24.0, ((0, 128),), (0, 1, 128, 5.5))
    return dict(homolog_embedding_tensor=homolog_embedding_tensor, standardizer_scale=standardizer_scale, standardizer_shift=standardizer_shift, first_operand_kernel=first_operand_kernel, left_projection_bias=left_projection_bias, second_operand_kernel=second_operand_kernel, right_projection_bias=right_projection_bias, output_weight_matrix=output_weight_matrix, output_bias_vector=output_bias_vector, pair_update_cotangent=pair_update_cotangent)


EPSILON = 1e-05

def normalize(features, standardizer_scale, standardizer_shift):
    average = lax.optimization_barrier(jnp.mean(features, axis=-1, keepdims=True))
    centred = features - average
    spread = lax.optimization_barrier(jnp.mean(centred * centred, axis=-1, keepdims=True))
    return centred * lax.rsqrt(spread + EPSILON) * standardizer_scale + standardizer_shift

def reference(homolog_embedding_tensor, standardizer_scale, standardizer_shift, first_operand_kernel, left_projection_bias, second_operand_kernel, right_projection_bias, output_weight_matrix, output_bias_vector, pair_update_cotangent):
    activations_fp32 = homolog_embedding_tensor.astype(jnp.float32)
    normed = normalize(activations_fp32, standardizer_scale, standardizer_shift).astype(jnp.bfloat16)
    normed32 = normed.astype(jnp.float32)
    left_proj = (jnp.einsum('sih,hc->sic', normed32, first_operand_kernel.astype(jnp.float32)) + left_projection_bias).astype(jnp.bfloat16)
    right_proj = (jnp.einsum('sih,hc->sic', normed32, second_operand_kernel.astype(jnp.float32)) + right_projection_bias).astype(jnp.bfloat16)
    scale_root = 1.0 / math.sqrt(POSITION_TOTAL)
    width = min(POSITION_TOTAL, 128)
    nblocks = POSITION_TOTAL // width
    right_blocks = jnp.moveaxis(right_proj.reshape(HOMOLOG_TOTAL, nblocks, width, HIDDEN_WIDTH), 1, 0)
    grad_blocks = jnp.moveaxis(pair_update_cotangent.reshape(POSITION_TOTAL, nblocks, width, CZ), 1, 0)
    left32 = left_proj.astype(jnp.float32)

    def advance(totals, pieces):
        w_total, b_total, a_total = totals
        right_piece, grad_piece = pieces
        right32 = right_piece.astype(jnp.float32)
        outer = (jnp.einsum('sic,sjd->ijcd', left32, right32) / HOMOLOG_TOTAL).astype(jnp.bfloat16)
        outer_flat = outer.reshape(POSITION_TOTAL * width, HIDDEN_WIDTH * HIDDEN_WIDTH)
        update = (jnp.dot(outer_flat, output_weight_matrix, preferred_element_type=jnp.float32) + output_bias_vector).astype(jnp.bfloat16)
        grad_flat = grad_piece.reshape(POSITION_TOTAL * width, CZ)
        outer_grad = (lax.dot_general(grad_flat, output_weight_matrix, (((1,), (1,)), ((), ())), preferred_element_type=jnp.float32) * scale_root).astype(jnp.bfloat16)
        w_total = w_total + lax.dot_general(outer_flat, grad_flat, (((0,), (0,)), ((), ())), preferred_element_type=jnp.float32)
        b_total = b_total + lax.optimization_barrier(jnp.sum(grad_flat.astype(jnp.float32), axis=0))
        grad4 = outer_grad.reshape(POSITION_TOTAL, width, HIDDEN_WIDTH, HIDDEN_WIDTH).astype(jnp.float32)
        a_total = a_total + jnp.einsum('ijcd,sjd->sic', grad4, right32) / HOMOLOG_TOTAL
        right_part = jnp.einsum('ijcd,sic->sjd', grad4, left32) / HOMOLOG_TOTAL
        return ((w_total, b_total, a_total), (update.reshape(POSITION_TOTAL, width, CZ), right_part))
    start = (jnp.zeros((HIDDEN_WIDTH * HIDDEN_WIDTH, CZ), jnp.float32), jnp.zeros((CZ,), jnp.float32), jnp.zeros((HOMOLOG_TOTAL, POSITION_TOTAL, HIDDEN_WIDTH), jnp.float32))
    totals, outputs = lax.scan(advance, start, (right_blocks, grad_blocks))
    w_total, b_total, left_grad = totals
    pair_representation_update = jnp.moveaxis(outputs[0], 0, 1).reshape(POSITION_TOTAL, POSITION_TOTAL, CZ)
    right_grad = jnp.moveaxis(outputs[1], 0, 1).reshape(HOMOLOG_TOTAL, POSITION_TOTAL, HIDDEN_WIDTH)
    output_weight_gradient = w_total * scale_root
    output_bias_gradient = b_total * scale_root
    highest = lax.Precision.HIGHEST
    left_weight_gradient = jnp.einsum('sih,sic->hc', normed32, left_grad, precision=highest)
    right_weight_gradient = jnp.einsum('sih,sic->hc', normed32, right_grad, precision=highest)
    left_bias_gradient = lax.optimization_barrier(jnp.sum(left_grad, axis=(0, 1)))
    right_bias_gradient = lax.optimization_barrier(jnp.sum(right_grad, axis=(0, 1)))
    normalized_gradient = jnp.einsum('sic,hc->sih', left_grad, first_operand_kernel.astype(jnp.float32), precision=highest)
    normalized_gradient = normalized_gradient + jnp.einsum('sic,hc->sih', right_grad, second_operand_kernel.astype(jnp.float32), precision=highest)
    unused, backward_function = jax.vjp(normalize, activations_fp32, standardizer_scale, standardizer_shift)
    alignment_gradient, norm_gain_gradient, norm_offset_gradient = backward_function(normalized_gradient)
    return (pair_representation_update, alignment_gradient, norm_gain_gradient, norm_offset_gradient, left_weight_gradient, left_bias_gradient, right_weight_gradient, right_bias_gradient, output_weight_gradient, output_bias_gradient)
```

```python
import math

import jax
import jax.numpy as jnp
from jax import lax
from jax.experimental import pallas as pl
from jax.experimental.pallas import tpu as pltpu
from jax.sharding import Mesh, PartitionSpec as P

EPSILON = 1e-05
F32 = jnp.float32
BF16 = jnp.bfloat16
S = 32
I = 8
C = 32
H = 256
Z = 128
J = 1024
NX, NZ, NY = 4, 8, 4
ND = NX * NZ * NY
Q = J // NX
SCALE = 1.0 / (math.sqrt(J) * S)
ROOT = 1.0 / math.sqrt(J)
NT = (((1,), (1,)), ((), ()))
TN = (((0,), (0,)), ((), ()))
PARAMS = pltpu.CompilerParams(vmem_limit_bytes=52 * 1024 * 1024)


def dot(a, b, dims=(((1,), (0,)), ((), ()))):
    return lax.dot_general(a, b, dims, preferred_element_type=F32)


def iota(shape, dim):
    return lax.broadcasted_iota(jnp.int32, shape, dim)


def one_hot(condition):
    return jnp.where(condition, 1.0, 0.0).astype(BF16)


def to_residue_major():
    row, col = iota((I * S, I * S), 0), iota((I * S, I * S), 1)
    return one_hot((row // S == col % I) & (row % S == col // I))


def split(value):
    high = value.astype(BF16)
    return high, (value - high.astype(F32)).astype(BF16)


def layer_norm_parts(x_ref):
    features = x_ref[...].astype(F32).reshape(S * I, H)
    average = jnp.mean(features, axis=-1, keepdims=True)
    centred = features - average
    spread = jnp.mean(centred * centred, axis=-1, keepdims=True)
    inverse = lax.rsqrt(spread + EPSILON)
    return centred, inverse


def rows_of(g_ref, quarter):
    start = pl.multiple_of(quarter * Q, Q)
    return jnp.concatenate([g_ref[i, pl.ds(start, Q), :] for i in range(I)], axis=1)


def first_kernel(
    x_ref, gain_ref, shift_ref, k1_ref, b1_ref, k2_ref, b2_ref, w_ref, g_ref,
    left_ref, right_ref, wd_ref, t_ref, p0_ref, p1_ref, p2_ref, p3_ref,
    w_scratch,
):
    plane = lax.axis_index("x")
    centred, inverse = layer_norm_parts(x_ref)
    normed = (centred * inverse * gain_ref[...] + shift_ref[...]).astype(BF16)
    left = (dot(normed, k1_ref[...]) + b1_ref[...]).astype(BF16)
    right = (dot(normed, k2_ref[...]) + b2_ref[...]).astype(BF16)
    left = dot(to_residue_major(), left).astype(BF16)
    left_ref[...] = left
    spread = dot(right, one_hot(iota((C, C * S), 0) == iota((C, C * S), 1) // S))
    keep = iota((S * I, C * S), 0) // I == iota((S * I, C * S), 1) % S
    kept = jnp.where(keep, spread, 0.0).astype(BF16)
    gather = one_hot(iota((I, S * I), 0) == iota((I, S * I), 1) % I)
    right_ref[...] = dot(gather, kept).astype(BF16)
    w_scratch[...] = w_ref[...].astype(F32)
    for d in range(C):
        wd_ref[:, d * Z : (d + 1) * Z] = w_scratch[pl.ds(d, C, stride=C), :].astype(BF16)
    for d in range(0, C, 2):
        block = dot(left, wd_ref[:, d * Z : (d + 2) * Z]).astype(BF16)
        for e in range(2):
            for i in range(I):
                t_ref[(d + e) * S : (d + e + 1) * S, i * Z : (i + 1) * Z] = block[
                    i * S : (i + 1) * S, e * Z : (e + 1) * Z
                ]
    for k, out in enumerate((p0_ref, p1_ref, p2_ref, p3_ref)):
        rows = rows_of(g_ref, (plane + k) % NX)
        out[...] = (dot(rows, t_ref[...], NT) * SCALE).astype(BF16)


def second_kernel(
    r0_ref, r1_ref, r2_ref, r3_ref, g_ref, left_ref, wd_ref, t_ref, bias_ref,
    x_ref, gain_ref, shift_ref, k1_ref, k2_ref, pieces_ref,
    update_ref, align_ref, pack_ref,
    rt_scratch, m_scratch, w_scratch,
):
    plane = lax.axis_index("x")
    bias = jnp.concatenate([bias_ref[...]] * I, axis=1)
    rights = (r0_ref, r1_ref, r2_ref, r3_ref)
    quarters = [(plane + NX - k) % NX for k in range(NX)]
    for k in range(NX):
        rt_scratch[:, k * Q : (k + 1) * Q] = rights[k][...].T
    for k in range(NX):
        block = (dot(rights[k][...], t_ref[...]) * (1.0 / S) + bias).astype(BF16)
        start = pl.multiple_of(quarters[k] * Q, Q)
        for i in range(I):
            update_ref[i, pl.ds(start, Q), :] = block[:, i * Z : (i + 1) * Z]
    bias_grad = jnp.zeros((1, Z), F32)
    for i in range(0, I, 2):
        pair = []
        for n in (i, i + 1):
            parts = [g_ref[n, pl.ds(pl.multiple_of(q * Q, Q), Q), :] for q in quarters]
            pair.append(jnp.concatenate(parts, axis=0))
            bias_grad = bias_grad + jnp.sum(pair[-1].astype(F32), axis=0, keepdims=True)
        u = dot(rt_scratch[...], jnp.concatenate(pair, axis=1)).astype(BF16)
        for e in range(2):
            for d in range(C):
                m_scratch[(i + e) * S : (i + e + 1) * S, d * Z : (d + 1) * Z] = u[
                    d * S : (d + 1) * S, e * Z : (e + 1) * Z
                ]
    left_grad = dot(m_scratch[...], wd_ref[...], NT) * SCALE
    w_part = dot(left_ref[...], m_scratch[...], TN) * SCALE
    for d in range(C):
        w_scratch[d * C : (d + 1) * C, :] = w_part[:, d * Z : (d + 1) * Z]
    total = jnp.sum(pieces_ref[...].astype(F32).reshape(NZ * NY, I, C * S), axis=0)
    high, low = split(total)
    scatter = one_hot(iota((S * I, I), 0) % I == iota((S * I, I), 1))
    keep = iota((S * I, C * S), 0) // I == iota((S * I, C * S), 1) % S
    fold = one_hot(iota((C * S, C), 0) // S == iota((C * S, C), 1))
    rg_high, rg_low = [
        dot(jnp.where(keep, dot(scatter, part), 0.0).astype(BF16), fold) for part in (high, low)
    ]
    right_grad = rg_high + rg_low
    high, low = split(left_grad)
    order = to_residue_major()
    left_grad = dot(order, high, TN) + dot(order, low, TN)
    lg_high, lg_low = split(left_grad)
    rg_high, rg_low = rg_high.astype(BF16), rg_low.astype(BF16)
    normed_grad = (
        dot(lg_high, k1_ref[...], NT)
        + dot(lg_low, k1_ref[...], NT)
        + dot(rg_high, k2_ref[...], NT)
        + dot(rg_low, k2_ref[...], NT)
    )
    centred, inverse = layer_norm_parts(x_ref)
    unit = centred * inverse
    normed = (unit * gain_ref[...] + shift_ref[...]).astype(BF16)
    unit_grad = normed_grad * gain_ref[...]
    mean_one = jnp.mean(unit_grad, axis=-1, keepdims=True)
    mean_two = jnp.mean(unit_grad * unit, axis=-1, keepdims=True)
    align_ref[...] = (inverse * (unit_grad - mean_one - unit * mean_two)).reshape(S, I, H)
    gain_grad = jnp.sum(normed_grad * unit, axis=0, keepdims=True)
    offset_grad = jnp.sum(normed_grad, axis=0, keepdims=True)
    both = jnp.concatenate([lg_high, rg_high, lg_low, rg_low], axis=1)
    weights = dot(both, normed, TN)
    weights = weights[: 2 * C] + weights[2 * C :]
    weights = jnp.concatenate([weights[:, :Z], weights[:, Z:]], axis=0)
    biases = jnp.sum(jnp.concatenate([left_grad, right_grad], axis=1), axis=0, keepdims=True)
    biases = jnp.concatenate([biases, jnp.zeros((1, Z - 2 * C), F32)], axis=1)
    row = iota((ND, Z), 0)
    others = jnp.zeros((ND, Z), F32)
    for n, value in enumerate(
        (gain_grad[:, :Z], gain_grad[:, Z:], offset_grad[:, :Z], offset_grad[:, Z:], biases, bias_grad)
    ):
        others = jnp.where(row == n, value, others)
    pack_ref[...] = packed(w_scratch[...].reshape(ND, 8, Z), weights, others)


def packed(w_rows, weights, others):
    where = iota((w_rows.shape[0], 8, Z), 1)
    block = jnp.zeros(where.shape, F32)
    n = 0
    for table in (weights, others):
        for half in split(table):
            block = jnp.where(where == n, half.astype(F32)[:, None, :], block)
            n += 1
    return jnp.concatenate([w_rows, block], axis=1).astype(BF16)


def sum_kernel(in_ref, out_ref):
    total = jnp.sum(in_ref[...].astype(F32), axis=0)
    block = packed(total[None, :8], total[8:9] + total[9:10], total[10:11] + total[11:12])
    out_ref[...] = jnp.broadcast_to(block, (ND, 16, Z))


def last_kernel(
    in_ref, gain_ref, offset_ref, lw_ref, lb_ref, rw_ref, rb_ref, w_ref, wb_ref, scratch, w_scratch
):
    blocks = in_ref[...].astype(F32)
    scratch[...] = blocks[:, 8:].reshape(ND * 8, Z)
    w_scratch[...] = blocks[:, :8].reshape(ND * 8, Z)
    for c in range(C):
        w_ref[c * C : (c + 1) * C, :] = w_scratch[pl.ds(c, C, stride=C), :]
    weights, others = [
        scratch[pl.ds(n, ND, stride=8), :] + scratch[pl.ds(n + 1, ND, stride=8), :] for n in (0, 2)
    ]
    flipped = weights.T
    lw_ref[:Z, :] = flipped[:, :C]
    lw_ref[Z:, :] = flipped[:, 2 * C : 3 * C]
    rw_ref[:Z, :] = flipped[:, C : 2 * C]
    rw_ref[Z:, :] = flipped[:, 3 * C :]
    gain_ref[:, :Z] = others[0:1]
    gain_ref[:, Z:] = others[1:2]
    offset_ref[:, :Z] = others[2:3]
    offset_ref[:, Z:] = others[3:4]
    lb_ref[...] = others[4:5, :C]
    rb_ref[...] = others[4:5, C : 2 * C]
    wb_ref[...] = others[5:6] * ROOT


def shape(dims, dtype):
    return jax.ShapeDtypeStruct(dims, dtype)


def shifted(array, step):
    return lax.ppermute(array, "x", [(n, (n + step) % NX) for n in range(NX)])


def per_device(x, gain, shift, k1, b1, k2, b2, w, bias, g):
    gain, shift, b1, b2, bias = [v.reshape(1, -1) for v in (gain, shift, b1, b2, bias)]
    left, right, wd, t, p0, p1, p2, p3 = pl.pallas_call(
        first_kernel,
        out_shape=(
            shape((I * S, C), BF16),
            shape((I, C * S), BF16),
            shape((C, C * Z), BF16),
            shape((C * S, I * Z), BF16),
        )
        + (shape((Q, C * S), BF16),) * NX,
        scratch_shapes=[pltpu.VMEM((C * C, Z), F32)],
        compiler_params=PARAMS,
        name="first",
    )(x, gain, shift, k1, b1, k2, b2, w, g)
    arrived = [shifted(p, k) for k, p in ((1, p1), (3, p3), (2, p2))]
    copies = jnp.broadcast_to(right[None], (NZ * NY, I, C * S)).reshape(Q, C * S)
    r0 = lax.all_to_all(copies, ("z", "y"), 0, 0, tiled=True)
    r1, r3, r2 = [shifted(r0, k) for k in (1, 3, 2)]
    own = p0.astype(F32)
    for p in arrived:
        own = own + p.astype(F32)
    pieces = lax.all_to_all(own.astype(BF16), ("z", "y"), 0, 0, tiled=True)
    update, align, pack = pl.pallas_call(
        second_kernel,
        out_shape=(
            shape((I, J, Z), BF16),
            shape((S, I, H), F32),
            shape((ND, 16, Z), BF16),
        ),
        scratch_shapes=[
            pltpu.VMEM((C * S, J), BF16),
            pltpu.VMEM((I * S, C * Z), BF16),
            pltpu.VMEM((C * C, Z), F32),
        ],
        compiler_params=PARAMS,
        name="second",
    )(r0, r1, r2, r3, g, left, wd, t, bias, x, gain, shift, k1, k2, pieces)
    parts = lax.all_to_all(pack, ("x", "z", "y"), 0, 0, tiled=True)
    block = pl.pallas_call(
        sum_kernel, out_shape=shape((ND, 16, Z), BF16), compiler_params=PARAMS, name="sum"
    )(parts)
    sums = lax.all_to_all(block, ("x", "z", "y"), 0, 0, tiled=True)
    gain_g, offset_g, lw, lb, rw, rb, w_g, wb = pl.pallas_call(
        last_kernel,
        out_shape=(
            shape((1, H), F32),
            shape((1, H), F32),
            shape((H, C), F32),
            shape((1, C), F32),
            shape((H, C), F32),
            shape((1, C), F32),
            shape((C * C, Z), F32),
            shape((1, Z), F32),
        ),
        scratch_shapes=[pltpu.VMEM((ND * 8, Z), F32), pltpu.VMEM((C * C, Z), F32)],
        compiler_params=PARAMS,
        name="last",
    )(sums)
    return (
        update,
        align,
        gain_g.reshape(H),
        offset_g.reshape(H),
        lw,
        lb.reshape(C),
        rw,
        rb.reshape(C),
        w_g,
        wb.reshape(Z),
    )


def solution(mesh):
    grid = Mesh(mesh.devices.reshape(NX, NZ, NY, 2), ("x", "z", "y", "dp"))
    dap = ("x", "z", "y")
    in_specs = (P("dp", dap, None),) + (P(),) * 8 + (P(("dp",) + dap, None, None),)
    out_specs = (
        P(("dp",) + dap, None, None),
        P("dp", dap, None),
        P("dp"),
        P("dp"),
        P("dp", None),
        P("dp"),
        P("dp", None),
        P("dp"),
        P("dp", None),
        P("dp"),
    )
    return jax.shard_map(
        per_device, mesh=grid, in_specs=in_specs, out_specs=out_specs, check_vma=False
    )
```

```python
import math

import jax
import jax.numpy as jnp
from jax import lax
from jax.experimental import pallas as pl
from jax.experimental.pallas import tpu as pltpu
from jax.sharding import Mesh, PartitionSpec as P

EPSILON = 1e-05
F32 = jnp.float32
BF16 = jnp.bfloat16
S = 32
I = 8
C = 32
H = 256
Z = 128
J = 1024
NX, NZ, NY = 4, 8, 4
ND = NX * NZ * NY
Q = J // NX
SCALE = 1.0 / (math.sqrt(J) * S)
ROOT = 1.0 / math.sqrt(J)
NT = (((1,), (1,)), ((), ()))
TN = (((0,), (0,)), ((), ()))
MIB = 1024 * 1024


def dot(a, b, dims=(((1,), (0,)), ((), ()))):
    return lax.dot_general(a, b, dims, preferred_element_type=F32)


def iota(shape, dim):
    return lax.broadcasted_iota(jnp.int32, shape, dim)


def one_hot(condition):
    return jnp.where(condition, 1.0, 0.0).astype(BF16)


def to_residue_major():
    row, col = iota((I * S, I * S), 0), iota((I * S, I * S), 1)
    return one_hot((row // S == col % I) & (row % S == col // I))


def split(value):
    high = value.astype(BF16)
    return high, (value - high.astype(F32)).astype(BF16)


def layer_norm_parts(x_ref):
    features = x_ref[...].astype(F32)
    average = jnp.mean(features, axis=-1, keepdims=True)
    centred = features - average
    spread = jnp.mean(centred * centred, axis=-1, keepdims=True)
    inverse = lax.rsqrt(spread + EPSILON)
    return centred, inverse


def rows_of(g_ref, quarter):
    start = pl.multiple_of(quarter * Q, Q)
    return jnp.concatenate([g_ref[i, pl.ds(start, Q), :] for i in range(I)], axis=1)


def copies_between(sources, targets, sems):
    return [pltpu.make_async_copy(a, b, sems.at[n]) for n, (a, b) in enumerate(zip(sources, targets))]


def first_kernel(*refs):
    inputs, outputs, held, (made, w_scratch, in_sems, out_sems) = (
        refs[:9], refs[9:17], refs[17:26], (refs[26:30], *refs[30:])
    )
    x_ref, gain_ref, shift_ref, k1_ref, b1_ref, k2_ref, b2_ref, w_ref, g_ref = held
    left_ref, copies_ref, wd_ref, t_ref = made
    partial_refs = outputs[4:]
    plane = lax.axis_index("x")
    loads = copies_between(inputs, held, in_sems)
    stores = copies_between(made, outputs, out_sems)
    for load in loads:
        load.start()
    for load in loads[:7]:
        load.wait()
    centred, inverse = layer_norm_parts(x_ref)
    normed = (centred * inverse * gain_ref[...] + shift_ref[...]).astype(BF16)
    left = (dot(normed, k1_ref[...], NT) + b1_ref[...]).astype(BF16)
    right = (dot(normed, k2_ref[...], NT) + b2_ref[...]).astype(BF16)
    left = dot(to_residue_major(), left).astype(BF16)
    left_ref[...] = left
    stores[0].start()
    spread = dot(right, one_hot(iota((C, C * S), 0) == iota((C, C * S), 1) // S))
    keep = iota((S * I, C * S), 0) // I == iota((S * I, C * S), 1) % S
    kept = jnp.where(keep, spread, 0.0).astype(BF16)
    gather = one_hot(iota((Q, S * I), 0) % I == iota((Q, S * I), 1) % I)
    copies_ref[...] = dot(gather, kept).astype(BF16)
    stores[1].start()
    loads[7].wait()
    w_scratch[...] = w_ref[...].astype(F32)
    for d in range(C):
        wd_ref[:, d * Z : (d + 1) * Z] = w_scratch[pl.ds(d, C, stride=C), :].astype(BF16)
    stores[2].start()
    for d in range(0, C, 2):
        block = dot(left, wd_ref[:, d * Z : (d + 2) * Z]).astype(BF16)
        for e in range(2):
            for i in range(I):
                t_ref[(d + e) * S : (d + e + 1) * S, i * Z : (i + 1) * Z] = block[
                    i * S : (i + 1) * S, e * Z : (e + 1) * Z
                ]
    stores[3].start()
    loads[8].wait()
    for k in (1, 3, 2, 0):
        rows = rows_of(g_ref, (plane + k) % NX)
        partial_refs[k][...] = (dot(rows, t_ref[...], NT) * SCALE).astype(BF16)
    for store in stores:
        store.wait()


def fold_kernel(a_ref, b_ref, c_ref, d_ref, out_ref):
    step = 16
    for n in range(0, Q, step):
        rows = pl.ds(n, step)
        total = a_ref[rows, :].astype(F32) + b_ref[rows, :].astype(F32)
        total = total + (c_ref[rows, :].astype(F32) + d_ref[rows, :].astype(F32))
        out_ref[rows, :] = total.astype(BF16)


def quarters_of():
    plane = lax.axis_index("x")
    return [(plane + NX - k) % NX for k in range(NX)]


def update_kernel(*refs):
    inputs, bias_ref, update_hbm, (held, update_ref, in_sems, out_sems) = (
        refs[:5], refs[5], refs[6], (refs[7:12], *refs[12:])
    )
    loads = copies_between(inputs, held, in_sems)
    for n in (4, 0, 1, 2, 3):
        loads[n].start()
    loads[4].wait()
    stores = []
    bias = jnp.concatenate([bias_ref[...]] * I, axis=1)
    for k, quarter in enumerate(quarters_of()):
        loads[k].wait()
        block = (dot(held[k][...], held[4][...]) * (1.0 / S) + bias).astype(BF16)
        rows = pl.ds(pl.multiple_of(quarter * Q, Q), Q)
        for i in range(I):
            update_ref[k, i] = block[:, i * Z : (i + 1) * Z]
        stores.append(pltpu.make_async_copy(update_ref.at[k], update_hbm.at[:, rows, :], out_sems.at[k]))
        stores[-1].start()
    for store in stores:
        store.wait()


def second_kernel(
    r0_any, r1_any, r2_any, r3_any, g_hbm, wd_hbm, left_ref,
    left_grad_ref, w_part_ref, bias_grad_ref,
    r0_ref, r1_ref, r2_ref, r3_ref, g_ref, wd_ref, rt_scratch, m_scratch, sems,
):
    quarters = quarters_of()
    sources = (r0_any, r1_any, r2_any, r3_any, g_hbm, wd_hbm)
    held = (r0_ref, r1_ref, r2_ref, r3_ref, g_ref, wd_ref)
    loads = copies_between(sources, held, sems)
    for load in loads:
        load.start()
    for k in range(NX):
        loads[k].wait()
        rt_scratch[:, k * Q : (k + 1) * Q] = held[k][...].T
    loads[4].wait()
    bias_grad = jnp.zeros((1, Z), F32)
    for i in range(0, I, 2):
        pair = []
        for n in (i, i + 1):
            parts = [g_ref[n, pl.ds(pl.multiple_of(q * Q, Q), Q), :] for q in quarters]
            pair.append(jnp.concatenate(parts, axis=0))
            bias_grad = bias_grad + jnp.sum(pair[-1].astype(F32), axis=0, keepdims=True)
        u = dot(rt_scratch[...], jnp.concatenate(pair, axis=1)).astype(BF16)
        for e in range(2):
            for d in range(C):
                m_scratch[(i + e) * S : (i + e + 1) * S, d * Z : (d + 1) * Z] = u[
                    d * S : (d + 1) * S, e * Z : (e + 1) * Z
                ]
    bias_grad_ref[...] = bias_grad
    loads[5].wait()
    left_grad_ref[...] = dot(m_scratch[...], wd_ref[...], NT) * SCALE
    w_part = dot(left_ref[...], m_scratch[...], TN) * SCALE
    for d in range(C):
        w_part_ref[d] = w_part[:, d * Z : (d + 1) * Z].astype(BF16)


def third_kernel(
    left_grad_ref, w_hbm, bias_grad_ref, x_ref, gain_ref, shift_ref, k1_ref, k2_ref, pieces_ref,
    align_ref, pack_ref, w_ref, sem,
):
    load = pltpu.make_async_copy(w_hbm, w_ref, sem)
    load.start()
    total = jnp.sum(pieces_ref[...].astype(F32).reshape(NZ * NY, I, C * S), axis=0)
    high, low = split(total)
    scatter = one_hot(iota((S * I, I), 0) % I == iota((S * I, I), 1))
    keep = iota((S * I, C * S), 0) // I == iota((S * I, C * S), 1) % S
    fold = one_hot(iota((C * S, C), 0) // S == iota((C * S, C), 1))
    rg_high, rg_low = [
        dot(jnp.where(keep, dot(scatter, part), 0.0).astype(BF16), fold) for part in (high, low)
    ]
    right_grad = rg_high + rg_low
    high, low = split(left_grad_ref[...])
    order = to_residue_major()
    left_grad = dot(order, high, TN) + dot(order, low, TN)
    lg_high, lg_low = split(left_grad)
    rg_high, rg_low = rg_high.astype(BF16), rg_low.astype(BF16)
    normed_grad = (
        dot(lg_high, k1_ref[...])
        + dot(lg_low, k1_ref[...])
        + dot(rg_high, k2_ref[...])
        + dot(rg_low, k2_ref[...])
    )
    centred, inverse = layer_norm_parts(x_ref)
    unit = centred * inverse
    normed = (unit * gain_ref[...] + shift_ref[...]).astype(BF16)
    unit_grad = normed_grad * gain_ref[...]
    mean_one = jnp.mean(unit_grad, axis=-1, keepdims=True)
    mean_two = jnp.mean(unit_grad * unit, axis=-1, keepdims=True)
    align_ref[...] = inverse * (unit_grad - mean_one - unit * mean_two)
    gain_grad = jnp.sum(normed_grad * unit, axis=0, keepdims=True)
    offset_grad = jnp.sum(normed_grad, axis=0, keepdims=True)
    both = jnp.concatenate([lg_high, rg_high, lg_low, rg_low], axis=1)
    weights = dot(both, normed, TN)
    weights = weights[: 2 * C] + weights[2 * C :]
    weights = jnp.concatenate([weights[:, :Z], weights[:, Z:]], axis=0)
    biases = jnp.sum(jnp.concatenate([left_grad, right_grad], axis=1), axis=0, keepdims=True)
    biases = jnp.concatenate([biases, jnp.zeros((1, Z - 2 * C), F32)], axis=1)
    halves = (gain_grad[:, :Z], gain_grad[:, Z:], offset_grad[:, :Z], offset_grad[:, Z:])
    rest = jnp.concatenate(halves + (biases, bias_grad_ref[...], jnp.zeros((2, Z), F32)), axis=0)
    tiles = weights.reshape(16, 1, 8, Z)
    small = jnp.concatenate([tiles, tiles], axis=1).reshape(32, 8, Z)
    block, row = iota(small.shape, 0), iota(small.shape, 1)
    rest = jnp.concatenate([rest[4:], rest[:4]], axis=0)[None]
    small = jnp.where(block % 2 == row // 4, small, jnp.where(block < 2, rest, 0.0))
    load.wait()
    pack_ref[...] = packed(w_ref[...].astype(F32), small)


def packed(w_rows, small):
    high = small.astype(BF16).astype(F32)
    return jnp.concatenate([w_rows, high, small - high], axis=1).astype(BF16)


def sum_kernel(in_ref, out_ref):
    total = jnp.sum(in_ref[...].astype(F32), axis=0)
    out_ref[...] = jnp.concatenate([total[:32], total[32:40] + total[40:]], axis=0)


def spread_kernel(a_ref, b_ref, c_ref, d_ref, out_ref):
    total = a_ref[...] + b_ref[...] + (c_ref[...] + d_ref[...])
    out_ref[...] = jnp.broadcast_to(packed(total[None, :32], total[None, 32:]), (32, 48, Z))


def last_kernel(
    in_ref, gain_ref, offset_ref, lw_ref, lb_ref, rw_ref, rb_ref, w_ref, wb_ref, w_scratch
):
    blocks = in_ref[...].astype(F32)
    w_scratch[...] = blocks[:, :32].reshape(C * C, Z)
    for c in range(C):
        w_ref[c * C : (c + 1) * C, :] = w_scratch[pl.ds(c, C, stride=C), :]
    small = blocks[:, 32:40] + blocks[:, 40:]
    pairs = small.reshape(16, 2, 8, Z)
    weights = jnp.where(iota((16, 8, Z), 1) < 4, pairs[:, 0], pairs[:, 1]).reshape(Z, Z)
    first, second = small[0], small[1]
    lw_ref[:, :Z] = weights[:C]
    lw_ref[:, Z:] = weights[2 * C : 3 * C]
    rw_ref[:, :Z] = weights[C : 2 * C]
    rw_ref[:, Z:] = weights[3 * C :]
    gain_ref[:, :Z] = first[4:5]
    gain_ref[:, Z:] = first[5:6]
    offset_ref[:, :Z] = first[6:7]
    offset_ref[:, Z:] = first[7:8]
    lb_ref[...] = second[0:1, :C]
    rb_ref[...] = second[0:1, C : 2 * C]
    wb_ref[...] = second[1:2] * ROOT


def shape(dims, dtype):
    return jax.ShapeDtypeStruct(dims, dtype)


HBM = pl.BlockSpec(memory_space=pltpu.HBM)
VMEM = pl.BlockSpec(memory_space=pltpu.VMEM)


def in_hbm(array):
    return pltpu.with_memory_space_constraint(array, pltpu.HBM)


def in_vmem(*arrays):
    return [pltpu.with_memory_space_constraint(v, pltpu.VMEM) for v in arrays]


def shifted(array, step):
    return lax.ppermute(array, "x", [(n, (n + step) % NX) for n in range(NX)])


def call(body, name, mib, out_shape, scratch=(), **more):
    params = pltpu.CompilerParams(vmem_limit_bytes=mib * MIB)
    return pl.pallas_call(
        body, out_shape=out_shape, scratch_shapes=list(scratch), compiler_params=params, name=name, **more
    )


def exchange(array):
    return lax.all_to_all(array, ("z", "y"), 0, 0, tiled=True)


def blocking_exchange(array):
    return lax.cond(lax.axis_index("x") < NX, exchange, jnp.zeros_like, array)


def per_device(x, gain, shift, k1, b1, k2, b2, w, bias, g):
    gain, shift, b1, b2, bias = [v.reshape(1, -1) for v in (gain, shift, b1, b2, bias)]
    x, k1, k2 = x.reshape(S * I, H), k1.T, k2.T
    inputs = (x, gain, shift, k1, b1, k2, b2, w, g)
    made = (
        ((I * S, C), BF16),
        ((Q, C * S), BF16),
        ((C, C * Z), BF16),
        ((C * S, I * Z), BF16),
    )
    left, copies, wd, t, p0, p1, p2, p3 = call(
        first_kernel,
        "first",
        16,
        tuple(pltpu.HBM(*v) for v in made) + (pltpu.VMEM((Q, C * S), BF16),) * NX,
        [pltpu.VMEM(v.shape, v.dtype) for v in inputs]
        + [pltpu.VMEM(*v) for v in made]
        + [pltpu.VMEM((C * C, Z), F32), pltpu.SemaphoreType.DMA((len(inputs),))]
        + [pltpu.SemaphoreType.DMA((len(made),))],
        in_specs=[HBM] * len(inputs),
        out_specs=[HBM] * len(made) + [VMEM] * NX,
    )(*[in_hbm(v) for v in inputs])
    arrived = [shifted(p, k) for k, p in ((1, p1), (3, p3), (2, p2))]
    r0 = blocking_exchange(copies)
    r1, r3, r2 = [shifted(r0, k) for k in (1, 3, 2)]
    quarter = ((Q, C * S), BF16)
    own = call(fold_kernel, "fold", 8, shape(*quarter))(*in_vmem(p0, *arrived))
    pieces = exchange(own)
    r0, r1, r2, r3 = [in_hbm(v) for v in (r0, r1, r2, r3)]
    left_grad, w_part, bias_grad = call(
        second_kernel,
        "second",
        16,
        (shape((I * S, C), F32), pltpu.HBM((C, C, Z), BF16), shape((1, Z), F32)),
        [pltpu.VMEM(*quarter)] * NX
        + [pltpu.VMEM(g.shape, BF16), pltpu.VMEM(wd.shape, BF16)]
        + [pltpu.VMEM((C * S, J), BF16), pltpu.VMEM((I * S, C * Z), BF16), pltpu.SemaphoreType.DMA((6,))],
        in_specs=[HBM] * (NX + 2) + [VMEM],
        cost_estimate=pl.CostEstimate(flops=100_000_000_000, bytes_accessed=0, transcendentals=0),
    )(r0, r1, r2, r3, in_hbm(g), in_hbm(wd), left)
    align, pack = call(
        third_kernel,
        "third",
        12,
        (shape((S * I, H), F32), shape((32, 48, Z), BF16)),
        [pltpu.VMEM((C, C, Z), BF16), pltpu.SemaphoreType.DMA],
        in_specs=[VMEM, HBM] + [VMEM] * 7,
    )(left_grad, in_hbm(w_part), bias_grad, x, gain, shift, k1, k2, pieces)
    parts = exchange(pack)
    update = call(
        update_kernel,
        "update",
        12,
        pltpu.HBM((I, J, Z), BF16),
        [pltpu.VMEM(*quarter)] * NX
        + [pltpu.VMEM(t.shape, BF16), pltpu.VMEM((NX, I, Q, Z), BF16)]
        + [pltpu.SemaphoreType.DMA((5,)), pltpu.SemaphoreType.DMA((NX,))],
        in_specs=[HBM] * (NX + 1) + [VMEM],
        out_specs=HBM,
    )(r0, r1, r2, r3, in_hbm(t), bias)
    mine = call(sum_kernel, "sum", 8, shape((40, Z), F32))(parts)
    others = [shifted(mine, k) for k in (1, 3, 2)]
    block = call(spread_kernel, "spread", 8, shape((32, 48, Z), BF16))(mine, *others)
    sums = exchange(block)
    gain_g, offset_g, lw, lb, rw, rb, w_g, wb = call(
        last_kernel,
        "last",
        8,
        (
            shape((1, H), F32),
            shape((1, H), F32),
            shape((C, H), F32),
            shape((1, C), F32),
            shape((C, H), F32),
            shape((1, C), F32),
            shape((C * C, Z), F32),
            shape((1, Z), F32),
        ),
        [pltpu.VMEM((C * C, Z), F32)],
    )(sums)
    return (
        update,
        align.reshape(S, I, H),
        gain_g.reshape(H),
        offset_g.reshape(H),
        lw.T,
        lb.reshape(C),
        rw.T,
        rb.reshape(C),
        w_g,
        wb.reshape(Z),
    )


def solution(mesh):
    grid = Mesh(mesh.devices.reshape(NX, NZ, NY, 2), ("x", "z", "y", "dp"))
    dap = ("x", "z", "y")
    in_specs = (P("dp", dap, None),) + (P(),) * 8 + (P(("dp",) + dap, None, None),)
    out_specs = (
        P(("dp",) + dap, None, None),
        P("dp", dap, None),
        P("dp"),
        P("dp"),
        P("dp", None),
        P("dp"),
        P("dp", None),
        P("dp"),
        P("dp", None),
        P("dp"),
    )
    return jax.shard_map(
        per_device, mesh=grid, in_specs=in_specs, out_specs=out_specs, check_vma=False
    )
```

```python
import itertools
import math

import jax
import jax.numpy as jnp
from jax import lax
from jax.experimental import pallas as pl
from jax.experimental.pallas import tpu as pltpu
from jax.sharding import Mesh, PartitionSpec as P

EPSILON = 1e-05
F32 = jnp.float32
BF16 = jnp.bfloat16
S = 32
I = 8
C = 32
H = 256
Z = 128
J = 1024
NX, NZ, NY = 4, 8, 4
NP = NX * NY
WR = C * C // NP
G = NZ * I
Q = J // NX
SCALE = 1.0 / (math.sqrt(J) * S)
ROOT = 1.0 / math.sqrt(J)
NT = (((1,), (1,)), ((), ()))
TN = (((0,), (0,)), ((), ()))
MIB = 1024 * 1024


def dot(a, b, dims=(((1,), (0,)), ((), ()))):
    return lax.dot_general(a, b, dims, preferred_element_type=F32)


def iota(shape, dim):
    return lax.broadcasted_iota(jnp.int32, shape, dim)


def one_hot(condition):
    return jnp.where(condition, 1.0, 0.0).astype(BF16)


def to_residue_major():
    row, col = iota((I * S, I * S), 0), iota((I * S, I * S), 1)
    return one_hot((row // S == col % I) & (row % S == col // I))


def split(value):
    high = value.astype(BF16)
    return high, (value - high.astype(F32)).astype(BF16)


def layer_norm_parts(x_ref):
    features = x_ref[...].astype(F32)
    average = jnp.mean(features, axis=-1, keepdims=True)
    centred = features - average
    spread = jnp.mean(centred * centred, axis=-1, keepdims=True)
    inverse = lax.rsqrt(spread + EPSILON)
    return centred, inverse


def places():
    core, x, y = lax.axis_index("dp"), lax.axis_index("x"), lax.axis_index("y")
    across = Q - I
    return x + (y - x) * core, y + (x - y) * core, Q - across * core, I + across * core


def block_rows(k, n):
    own, _, long_stride, short_stride = places()
    start = (own + NX - k) % NX * long_stride + n // NY * (NY * I) + n % NY * short_stride
    return pl.ds(pl.multiple_of(start, I), I)


def rows_of(g_ref, k):
    return jnp.concatenate([g_ref[i, k * Q : (k + 1) * Q, :] for i in range(I)], axis=1)


def copies_between(sources, targets, sems):
    return [pltpu.make_async_copy(a, b, sems.at[n]) for n, (a, b) in enumerate(zip(sources, targets))]


def first_kernel(*refs):
    inputs, outputs, held, (made, w_scratch, g_scratch, in_sems, out_sems) = (
        refs[:9], refs[9:18], refs[18:27], (refs[27:32], *refs[32:])
    )
    x_ref, gain_ref, shift_ref, k1_ref, b1_ref, k2_ref, b2_ref, w_ref, g_ref = held
    left_ref, copies_ref, wd_ref, t_ref, ordered_ref = made
    partial_refs = outputs[5:]
    loads = copies_between(inputs, held, in_sems)
    stores = copies_between(made, outputs, out_sems)
    for load in loads:
        load.start()
    for load in loads[:7]:
        load.wait()
    centred, inverse = layer_norm_parts(x_ref)
    normed = (centred * inverse * gain_ref[...] + shift_ref[...]).astype(BF16)
    left = (dot(normed, k1_ref[...], NT) + b1_ref[...]).astype(BF16)
    right = (dot(normed, k2_ref[...], NT) + b2_ref[...]).astype(BF16)
    left = dot(to_residue_major(), left).astype(BF16)
    left_ref[...] = left
    stores[0].start()
    spread = dot(right, one_hot(iota((C, C * S), 0) == iota((C, C * S), 1) // S))
    keep = iota((S * I, C * S), 0) // I == iota((S * I, C * S), 1) % S
    kept = jnp.where(keep, spread, 0.0).astype(BF16)
    gather = one_hot(iota((G, S * I), 0) % I == iota((G, S * I), 1) % I)
    copies_ref[...] = dot(gather, kept).astype(BF16)
    stores[1].start()
    loads[7].wait()
    w_scratch[...] = w_ref[...].astype(F32)
    for d in range(C):
        wd_ref[:, d * Z : (d + 1) * Z] = w_scratch[pl.ds(d, C, stride=C), :].astype(BF16)
    stores[2].start()
    for d in range(0, C, 2):
        block = dot(left, wd_ref[:, d * Z : (d + 2) * Z]).astype(BF16)
        for e in range(2):
            for i in range(I):
                t_ref[(d + e) * S : (d + e + 1) * S, i * Z : (i + 1) * Z] = block[
                    i * S : (i + 1) * S, e * Z : (e + 1) * Z
                ]
    stores[3].start()
    loads[8].wait()
    g_scratch[...] = g_ref[...].astype(F32)
    for k in range(NX):
        for n in range(0, NZ * NY, 2):
            pair = [g_scratch[:, block_rows(k, m), :] for m in (n, n + 1)]
            start = k * Q + n * I
            ordered_ref[:, start : start + 2 * I, :] = jnp.concatenate(pair, axis=1).astype(BF16)
    stores[4].start()
    for k in range(NX):
        rows = rows_of(ordered_ref, (NX - k) % NX)
        partial_refs[k][...] = (dot(rows, t_ref[...], NT) * SCALE).astype(BF16)
    for store in stores:
        store.wait()


def added(refs, rows):
    a, b, c, d = [ref[rows, :].astype(F32) for ref in refs]
    return (a + b) + (c + d)


def fold_kernel(*refs):
    inputs, outputs, total = refs[:4], refs[4:8], refs[8]
    line = places()[1]
    for n in range(0, Q, 16):
        rows = pl.ds(n, 16)
        total[rows, :] = added(inputs, rows)
    for k, out in enumerate(outputs):
        first = (line + k) % NY * I
        for z in range(0, NZ, 2):
            pair = [total[pl.ds(pl.multiple_of(n * NY * I + first, I), I), :] for n in (z, z + 1)]
            out[z * I : (z + 2) * I, :] = jnp.concatenate(pair, axis=0).astype(BF16)


def add_kernel(*refs):
    for n in range(0, G, 16):
        rows = pl.ds(n, 16)
        refs[4][rows, :] = added(refs[:4], rows)


def arrange_kernel(*refs):
    inputs, out_ref, total = refs[:4], refs[5], refs[6]
    line = places()[1]
    for k, ref in enumerate(inputs):
        first = (line + NY - k) % NY * I
        for z in range(0, NZ, 2):
            rows = ref[z * I : (z + 2) * I, :].astype(F32)
            for e in range(2):
                start = pl.multiple_of((z + e) * NY * I + first, I)
                total[pl.ds(start, I), :] = rows[e * I : (e + 1) * I]
    for n in range(0, Q, 16):
        out_ref[pl.ds(n, 16), :] = total[pl.ds(n, 16), :].astype(BF16)


def update_kernel(
    r0_ref, r1_ref, r2_ref, r3_ref, t_hbm, bias_ref, update_hbm, t_ref, update_ref, scratch, sem, sems
):
    load = pltpu.make_async_copy(t_hbm, t_ref, sem)
    load.start()
    load.wait()
    bias = jnp.concatenate([bias_ref[...]] * I, axis=1)
    for k, right in enumerate((r0_ref, r1_ref, r2_ref, r3_ref)):
        block = dot(right[...], t_ref[...]) * (1.0 / S) + bias
        for n in range(NZ * NY):
            scratch[block_rows(k, n), :] = block[n * I : (n + 1) * I]
    stores = []
    for k in range(NX):
        rows = pl.ds(k * Q, Q)
        for i in range(I):
            update_ref[i, rows, :] = scratch[rows, i * Z : (i + 1) * Z].astype(BF16)
        stores.append(pltpu.make_async_copy(update_ref.at[:, rows, :], update_hbm.at[:, rows, :], sems.at[k]))
        stores[-1].start()
    for store in stores:
        store.wait()


def second_kernel(
    r0_ref, r1_ref, r2_ref, r3_ref, g_hbm, wd_hbm, left_ref,
    left_grad_ref, w_part_ref, bias_grad_ref,
    g_ref, wd_ref, rt_scratch, m_scratch, sems,
):
    loads = copies_between((g_hbm, wd_hbm), (g_ref, wd_ref), sems)
    for load in loads:
        load.start()
    for k, right in enumerate((r0_ref, r1_ref, r2_ref, r3_ref)):
        rt_scratch[:, k * Q : (k + 1) * Q] = right[...].T
    loads[0].wait()
    bias_grad = jnp.zeros((1, Z), F32)
    for i in range(0, I, 2):
        pair = []
        for n in (i, i + 1):
            pair.append(g_ref[n])
            bias_grad = bias_grad + jnp.sum(pair[-1].astype(F32), axis=0, keepdims=True)
        u = dot(rt_scratch[...], jnp.concatenate(pair, axis=1)).astype(BF16)
        for e in range(2):
            for d in range(C):
                m_scratch[(i + e) * S : (i + e + 1) * S, d * Z : (d + 1) * Z] = u[
                    d * S : (d + 1) * S, e * Z : (e + 1) * Z
                ]
    bias_grad_ref[...] = bias_grad
    loads[1].wait()
    left_grad_ref[...] = dot(m_scratch[...], wd_ref[...], NT) * SCALE
    w_part = dot(left_ref[...], m_scratch[...], TN) * SCALE
    for d in range(C):
        w_part_ref[d] = w_part[:, d * Z : (d + 1) * Z].astype(BF16)


def third_kernel(
    left_grad_ref, w_hbm, bias_grad_ref, x_ref, gain_ref, shift_ref, k1_ref, k2_ref, pieces_ref,
    align_ref, pack_ref, w_ref, sem,
):
    load = pltpu.make_async_copy(w_hbm, w_ref, sem)
    load.start()
    total = jnp.sum(pieces_ref[...].astype(F32).reshape(NZ, I, C * S), axis=0)
    high, low = split(total)
    scatter = one_hot(iota((S * I, I), 0) % I == iota((S * I, I), 1))
    keep = iota((S * I, C * S), 0) // I == iota((S * I, C * S), 1) % S
    fold = one_hot(iota((C * S, C), 0) // S == iota((C * S, C), 1))
    rg_high, rg_low = [
        dot(jnp.where(keep, dot(scatter, part), 0.0).astype(BF16), fold) for part in (high, low)
    ]
    right_grad = rg_high + rg_low
    high, low = split(left_grad_ref[...])
    order = to_residue_major()
    left_grad = dot(order, high, TN) + dot(order, low, TN)
    lg_high, lg_low = split(left_grad)
    rg_high, rg_low = rg_high.astype(BF16), rg_low.astype(BF16)
    normed_grad = (
        dot(lg_high, k1_ref[...])
        + dot(lg_low, k1_ref[...])
        + dot(rg_high, k2_ref[...])
        + dot(rg_low, k2_ref[...])
    )
    centred, inverse = layer_norm_parts(x_ref)
    unit = centred * inverse
    normed = (unit * gain_ref[...] + shift_ref[...]).astype(BF16)
    unit_grad = normed_grad * gain_ref[...]
    mean_one = jnp.mean(unit_grad, axis=-1, keepdims=True)
    mean_two = jnp.mean(unit_grad * unit, axis=-1, keepdims=True)
    align_ref[...] = inverse * (unit_grad - mean_one - unit * mean_two)
    gain_grad = jnp.sum(normed_grad * unit, axis=0, keepdims=True)
    offset_grad = jnp.sum(normed_grad, axis=0, keepdims=True)
    both = jnp.concatenate([lg_high, rg_high, lg_low, rg_low], axis=1)
    weights = dot(both, normed, TN)
    weights = weights[: 2 * C] + weights[2 * C :]
    weights = jnp.concatenate([weights[:, :Z], weights[:, Z:]], axis=0)
    biases = jnp.sum(jnp.concatenate([left_grad, right_grad], axis=1), axis=0, keepdims=True)
    biases = jnp.concatenate([biases, jnp.zeros((1, Z - 2 * C), F32)], axis=1)
    halves = (gain_grad[:, :Z], gain_grad[:, Z:], offset_grad[:, :Z], offset_grad[:, Z:])
    rest = jnp.concatenate(halves + (biases, bias_grad_ref[...], jnp.zeros((2, Z), F32)), axis=0)
    rest = jnp.where(iota((NP, 8, Z), 0) == 0, rest[None], 0.0)
    small = jnp.concatenate([weights.reshape(NP, 8, Z), rest], axis=1)
    load.wait()
    pack_ref[...] = packed(w_ref[...].astype(F32).reshape(NP, WR, Z), small)


def packed(w_rows, small):
    high = small.astype(BF16).astype(F32)
    return jnp.concatenate([w_rows, high, small - high], axis=1).astype(BF16)


def sum_kernel(in_ref, out_ref):
    total = jnp.sum(in_ref[...].astype(F32), axis=0)
    total = jnp.concatenate([total[:WR], total[WR : WR + 16] + total[WR + 16 :]], axis=0)
    out_ref[...] = jnp.broadcast_to(total[None], out_ref.shape)


def spread_kernel(in_ref, out_ref):
    total = jnp.sum(in_ref[...], axis=0)[None]
    out_ref[...] = jnp.broadcast_to(packed(total[:, :WR], total[:, WR:]), out_ref.shape)


def last_kernel(
    in_ref, gain_ref, offset_ref, lw_ref, lb_ref, rw_ref, rb_ref, w_ref, wb_ref, w_scratch
):
    blocks = in_ref[...].astype(F32)
    w_scratch[...] = blocks[:, :WR].reshape(C * C, Z)
    for c in range(C):
        w_ref[c * C : (c + 1) * C, :] = w_scratch[pl.ds(c, C, stride=C), :]
    small = blocks[:, WR : WR + 16] + blocks[:, WR + 16 :]
    weights = small[:, :8].reshape(Z, Z)
    rest = small[0, 8:]
    lw_ref[:, :Z] = weights[:C]
    lw_ref[:, Z:] = weights[2 * C : 3 * C]
    rw_ref[:, :Z] = weights[C : 2 * C]
    rw_ref[:, Z:] = weights[3 * C :]
    gain_ref[:, :Z] = rest[0:1]
    gain_ref[:, Z:] = rest[1:2]
    offset_ref[:, :Z] = rest[2:3]
    offset_ref[:, Z:] = rest[3:4]
    lb_ref[...] = rest[4:5, :C]
    rb_ref[...] = rest[4:5, C : 2 * C]
    wb_ref[...] = rest[5:6] * ROOT


def shape(dims, dtype):
    return jax.ShapeDtypeStruct(dims, dtype)


LATE = pl.CostEstimate(flops=100_000_000_000, bytes_accessed=0, transcendentals=0)
HBM = pl.BlockSpec(memory_space=pltpu.HBM)
VMEM = pl.BlockSpec(memory_space=pltpu.VMEM)


def in_hbm(array):
    return pltpu.with_memory_space_constraint(array, pltpu.HBM)


def in_vmem(*arrays):
    return [pltpu.with_memory_space_constraint(v, pltpu.VMEM) for v in arrays]


def ring(step, long):
    def number(x, z, y, core):
        return ((x % NX * NZ + z) * NY + y % NY) * 2 + core

    pairs = []
    for x, z, y, core in itertools.product(range(NX), range(NZ), range(NY), range(2)):
        by_x = long == (core == 0)
        target = number(x + step * by_x, z, y + step * (not by_x), core)
        pairs.append((number(x, z, y, core), target))
    return pairs


def shifted(arrays, long):
    return [arrays[0]] + [
        lax.ppermute(arrays[k], ("x", "z", "y", "dp"), ring(k, long)) for k in (1, 2, 3)
    ]


def call(body, name, mib, out_shape, scratch=(), **more):
    params = pltpu.CompilerParams(vmem_limit_bytes=mib * MIB)
    return pl.pallas_call(
        body, out_shape=out_shape, scratch_shapes=list(scratch), compiler_params=params, name=name, **more
    )


def exchange(array, axes):
    return lax.all_to_all(array, axes, 0, 0, tiled=True)


def blocking_exchange(array, axes):
    return lax.cond(lax.axis_index("x") < NX, lambda v: exchange(v, axes), jnp.zeros_like, array)


def per_device(x, gain, shift, k1, b1, k2, b2, w, bias, g):
    gain, shift, b1, b2, bias = [v.reshape(1, -1) for v in (gain, shift, b1, b2, bias)]
    x, k1, k2 = x.reshape(S * I, H), k1.T, k2.T
    inputs = (x, gain, shift, k1, b1, k2, b2, w, g)
    made = (
        ((I * S, C), BF16),
        ((G, C * S), BF16),
        ((C, C * Z), BF16),
        ((C * S, I * Z), BF16),
        (g.shape, BF16),
    )
    left, copies, wd, t, ordered, p0, p1, p2, p3 = call(
        first_kernel,
        "first",
        24,
        tuple(pltpu.HBM(*v) for v in made) + (pltpu.VMEM((Q, C * S), BF16),) * NX,
        [pltpu.VMEM(v.shape, v.dtype) for v in inputs]
        + [pltpu.VMEM(*v) for v in made]
        + [pltpu.VMEM((C * C, Z), F32), pltpu.VMEM(g.shape, F32), pltpu.SemaphoreType.DMA((len(inputs),))]
        + [pltpu.SemaphoreType.DMA((len(made),))],
        in_specs=[HBM] * len(inputs),
        out_specs=[HBM] * len(made) + [VMEM] * NX,
    )(*[in_hbm(v) for v in inputs])
    quarter = ((Q, C * S), BF16)
    column = ((G, C * S), BF16)
    planes = shifted((p0, p1, p2, p3), True)
    near = blocking_exchange(copies, "z")
    lines = shifted([near] * NY, False)
    parts = call(
        fold_kernel, "fold", 8, (pltpu.VMEM(*column),) * NY, [pltpu.VMEM((Q, C * S), F32)]
    )(*in_vmem(*planes))
    sums = shifted(parts, False)
    r0 = call(arrange_kernel, "arrange", 8, pltpu.VMEM(*quarter), [pltpu.VMEM((Q, C * S), F32)])(
        *in_vmem(*lines, parts[0])
    )
    r0, r1, r2, r3 = in_vmem(*shifted([r0] * NX, True))
    own = call(add_kernel, "add", 8, shape((G, C * S), F32), cost_estimate=LATE)(*in_vmem(*sums))
    pieces = exchange(own, "z")
    left_grad, w_part, bias_grad = call(
        second_kernel,
        "second",
        16,
        (shape((I * S, C), F32), pltpu.HBM((C, C, Z), BF16), shape((1, Z), F32)),
        [pltpu.VMEM(g.shape, BF16), pltpu.VMEM(wd.shape, BF16)]
        + [pltpu.VMEM((C * S, J), BF16), pltpu.VMEM((I * S, C * Z), BF16), pltpu.SemaphoreType.DMA((2,))],
        in_specs=[VMEM] * NX + [HBM] * 2 + [VMEM],
        cost_estimate=LATE,
    )(r0, r1, r2, r3, in_hbm(ordered), in_hbm(wd), left)
    align, pack = call(
        third_kernel,
        "third",
        12,
        (shape((S * I, H), F32), shape((NP, WR + 32, Z), BF16)),
        [pltpu.VMEM((C, C, Z), BF16), pltpu.SemaphoreType.DMA],
        in_specs=[VMEM, HBM] + [VMEM] * 7,
    )(left_grad, in_hbm(w_part), bias_grad, x, gain, shift, k1, k2, pieces)
    parts = exchange(pack, ("x", "y"))
    update = call(
        update_kernel,
        "update",
        20,
        pltpu.HBM((I, J, Z), BF16),
        [pltpu.VMEM(t.shape, BF16), pltpu.VMEM((I, J, Z), BF16), pltpu.VMEM((J, I * Z), F32)]
        + [pltpu.SemaphoreType.DMA, pltpu.SemaphoreType.DMA((NX,))],
        in_specs=[VMEM] * NX + [HBM] + [VMEM],
        out_specs=HBM,
    )(r0, r1, r2, r3, in_hbm(t), bias)
    plane = call(sum_kernel, "sum", 8, shape((NZ, WR + 16, Z), F32))(parts)
    column = exchange(plane, "z")
    block = call(spread_kernel, "spread", 8, shape((NP, WR + 32, Z), BF16))(column)
    sums = exchange(block, ("x", "y"))
    gain_g, offset_g, lw, lb, rw, rb, w_g, wb = call(
        last_kernel,
        "last",
        8,
        (
            shape((1, H), F32),
            shape((1, H), F32),
            shape((C, H), F32),
            shape((1, C), F32),
            shape((C, H), F32),
            shape((1, C), F32),
            shape((C * C, Z), F32),
            shape((1, Z), F32),
        ),
        [pltpu.VMEM((C * C, Z), F32)],
    )(sums)
    return (
        update,
        align.reshape(S, I, H),
        gain_g.reshape(H),
        offset_g.reshape(H),
        lw.T,
        lb.reshape(C),
        rw.T,
        rb.reshape(C),
        w_g,
        wb.reshape(Z),
    )


def solution(mesh):
    grid = Mesh(mesh.devices.reshape(NX, NZ, NY, 2), ("x", "z", "y", "dp"))
    dap = ("x", "z", "y")
    in_specs = (P("dp", dap, None),) + (P(),) * 8 + (P(("dp",) + dap, None, None),)
    out_specs = (
        P(("dp",) + dap, None, None),
        P("dp", dap, None),
        P("dp"),
        P("dp"),
        P("dp", None),
        P("dp"),
        P("dp", None),
        P("dp"),
        P("dp", None),
        P("dp"),
    )
    return jax.shard_map(
        per_device, mesh=grid, in_specs=in_specs, out_specs=out_specs, check_vma=False
    )
```

```python
import itertools
import math

import jax
import jax.numpy as jnp
from jax import lax
from jax.experimental import pallas as pl
from jax.experimental.pallas import tpu as pltpu
from jax.sharding import Mesh, PartitionSpec as P

EPSILON = 1e-05
F32 = jnp.float32
BF16 = jnp.bfloat16
S = 32
I = 8
C = 32
H = 256
Z = 128
J = 1024
NX, NZ, NY = 4, 8, 4
NP = NX * NY
WR = C * C // NP
G = NZ * I
Q = J // NX
SCALE = 1.0 / (math.sqrt(J) * S)
ROOT = 1.0 / math.sqrt(J)
NT = (((1,), (1,)), ((), ()))
TN = (((0,), (0,)), ((), ()))
MIB = 1024 * 1024


def dot(a, b, dims=(((1,), (0,)), ((), ()))):
    return lax.dot_general(a, b, dims, preferred_element_type=F32)


def iota(shape, dim):
    return lax.broadcasted_iota(jnp.int32, shape, dim)


def one_hot(condition):
    return jnp.where(condition, 1.0, 0.0).astype(BF16)


def to_residue_major():
    row, col = iota((I * S, I * S), 0), iota((I * S, I * S), 1)
    return one_hot((row // S == col % I) & (row % S == col // I))


def split(value):
    high = value.astype(BF16)
    return high, (value - high.astype(F32)).astype(BF16)


def layer_norm_parts(x_ref):
    features = x_ref[...].astype(F32)
    average = jnp.mean(features, axis=-1, keepdims=True)
    centred = features - average
    spread = jnp.mean(centred * centred, axis=-1, keepdims=True)
    inverse = lax.rsqrt(spread + EPSILON)
    return centred, inverse


def places():
    core, x, y = lax.axis_index("dp"), lax.axis_index("x"), lax.axis_index("y")
    across = Q - I
    return x + (y - x) * core, y + (x - y) * core, Q - across * core, I + across * core


def block_rows(k, n):
    own, _, long_stride, short_stride = places()
    start = (own + NX - k) % NX * long_stride + n // NY * (NY * I) + n % NY * short_stride
    return pl.ds(pl.multiple_of(start, I), I)


def copies_between(sources, targets, sems):
    return [pltpu.make_async_copy(a, b, sems.at[n]) for n, (a, b) in enumerate(zip(sources, targets))]


def first_kernel(*refs):
    inputs, outputs, held, (made, w_scratch, g_scratch, in_sems, out_sems) = (
        refs[:9], refs[9:18], refs[18:27], (refs[27:32], *refs[32:])
    )
    x_ref, gain_ref, shift_ref, k1_ref, b1_ref, k2_ref, b2_ref, w_ref, g_ref = held
    left_ref, copies_ref, wd_ref, t_ref, ordered_ref = made
    partial_refs = outputs[5:]
    loads = copies_between(inputs, held, in_sems)
    stores = copies_between(made, outputs, out_sems)
    for load in loads:
        load.start()
    for load in loads[:7]:
        load.wait()
    centred, inverse = layer_norm_parts(x_ref)
    normed = (centred * inverse * gain_ref[...] + shift_ref[...]).astype(BF16)
    left = (dot(normed, k1_ref[...], NT) + b1_ref[...]).astype(BF16)
    right = (dot(normed, k2_ref[...], NT) + b2_ref[...]).astype(BF16)
    left = dot(to_residue_major(), left).astype(BF16)
    left_ref[...] = left
    stores[0].start()
    spread = dot(right, one_hot(iota((C, C * S), 0) == iota((C, C * S), 1) // S))
    keep = iota((S * I, C * S), 0) // I == iota((S * I, C * S), 1) % S
    kept = jnp.where(keep, spread, 0.0).astype(BF16)
    gather = one_hot(iota((G, S * I), 0) % I == iota((G, S * I), 1) % I)
    copies_ref[...] = dot(gather, kept).astype(BF16)
    stores[1].start()
    loads[7].wait()
    w_scratch[...] = w_ref[...].astype(F32)
    for d in range(C):
        wd_ref[:, d * Z : (d + 1) * Z] = w_scratch[pl.ds(d, C, stride=C), :].astype(BF16)
    stores[2].start()
    for d in range(0, C, 2):
        block = dot(left, wd_ref[:, d * Z : (d + 2) * Z]).astype(BF16)
        for e in range(2):
            for i in range(I):
                t_ref[(d + e) * S : (d + e + 1) * S, i * Z : (i + 1) * Z] = block[
                    i * S : (i + 1) * S, e * Z : (e + 1) * Z
                ]
    stores[3].start()
    loads[8].wait()
    g_scratch[...] = g_ref[...].astype(F32)
    for k in range(NX):
        for n in range(0, NZ * NY, 2):
            pair = [g_scratch[:, block_rows(k, m), :] for m in (n, n + 1)]
            start = k * Q + n * I
            ordered_ref[:, start : start + 2 * I, :] = jnp.concatenate(pair, axis=1).astype(BF16)
    stores[4].start()
    rows = jnp.concatenate([ordered_ref[i] for i in range(I)], axis=1)
    whole = dot(rows, t_ref[...], NT) * SCALE
    for k in range(NX):
        start = (NX - k) % NX * Q
        partial_refs[k][...] = whole[start : start + Q].astype(BF16)
    for store in stores:
        store.wait()


def added(refs, rows):
    a, b, c, d = [ref[rows, :].astype(F32) for ref in refs]
    return (a + b) + (c + d)


def fold_kernel(*refs):
    inputs, outputs, total = refs[:4], refs[4:8], refs[8]
    line = places()[1]
    for n in range(0, Q, 16):
        rows = pl.ds(n, 16)
        total[rows, :] = added(inputs, rows)
    for k, out in enumerate(outputs):
        first = (line + k) % NY * I
        for z in range(0, NZ, 2):
            pair = [total[pl.ds(pl.multiple_of(n * NY * I + first, I), I), :] for n in (z, z + 1)]
            out[z * I : (z + 2) * I, :] = jnp.concatenate(pair, axis=0).astype(BF16)


def add_kernel(*refs):
    for n in range(0, G, 16):
        rows = pl.ds(n, 16)
        refs[4][rows, :] = added(refs[:4], rows)


def arrange_kernel(*refs):
    inputs, out_ref, total = refs[:4], refs[5], refs[6]
    line = places()[1]
    for k, ref in enumerate(inputs):
        first = (line + NY - k) % NY * I
        for z in range(0, NZ, 2):
            rows = ref[z * I : (z + 2) * I, :].astype(F32)
            for e in range(2):
                start = pl.multiple_of((z + e) * NY * I + first, I)
                total[pl.ds(start, I), :] = rows[e * I : (e + 1) * I]
    for n in range(0, Q, 16):
        out_ref[pl.ds(n, 16), :] = total[pl.ds(n, 16), :].astype(BF16)


def update_kernel(
    r0_ref, r1_ref, r2_ref, r3_ref, t_hbm, bias_ref, update_hbm, t_ref, update_ref, scratch, sem, sems
):
    load = pltpu.make_async_copy(t_hbm, t_ref, sem)
    load.start()
    load.wait()
    bias = jnp.concatenate([bias_ref[...]] * I, axis=1)
    for k, right in enumerate((r0_ref, r1_ref, r2_ref, r3_ref)):
        block = dot(right[...], t_ref[...]) * (1.0 / S) + bias
        for n in range(NZ * NY):
            scratch[block_rows(k, n), :] = block[n * I : (n + 1) * I]
    stores = []
    for k in range(NX):
        rows = pl.ds(k * Q, Q)
        for i in range(I):
            update_ref[i, rows, :] = scratch[rows, i * Z : (i + 1) * Z].astype(BF16)
        stores.append(pltpu.make_async_copy(update_ref.at[:, rows, :], update_hbm.at[:, rows, :], sems.at[k]))
        stores[-1].start()
    for store in stores:
        store.wait()


def second_kernel(
    r0_ref, r1_ref, r2_ref, r3_ref, g_hbm, wd_hbm, left_ref,
    left_grad_ref, w_part_ref, bias_grad_ref,
    g_ref, wd_ref, rt_scratch, m_scratch, sems,
):
    loads = copies_between((g_hbm, wd_hbm), (g_ref, wd_ref), sems)
    for load in loads:
        load.start()
    for k, right in enumerate((r0_ref, r1_ref, r2_ref, r3_ref)):
        rt_scratch[: C * S, k * Q : (k + 1) * Q] = right[...].T
    loads[0].wait()
    rt_scratch[C * S :, :] = jnp.ones((16, J), BF16)
    bias_grad = jnp.zeros((1, Z), F32)
    for i in range(0, I, 2):
        pair = []
        for n in (i, i + 1):
            pair.append(g_ref[n])
        u = dot(rt_scratch[...], jnp.concatenate(pair, axis=1))
        bias_grad = bias_grad + (u[C * S : C * S + 1, :Z] + u[C * S : C * S + 1, Z:])
        u = u[: C * S].astype(BF16)
        for e in range(2):
            for d in range(C):
                m_scratch[(i + e) * S : (i + e + 1) * S, d * Z : (d + 1) * Z] = u[
                    d * S : (d + 1) * S, e * Z : (e + 1) * Z
                ]
    bias_grad_ref[...] = bias_grad
    loads[1].wait()
    left_grad_ref[...] = dot(m_scratch[...], wd_ref[...], NT) * SCALE
    w_part = dot(left_ref[...], m_scratch[...], TN) * SCALE
    for d in range(C):
        w_part_ref[d] = w_part[:, d * Z : (d + 1) * Z].astype(BF16)


def third_kernel(
    left_grad_ref, w_hbm, bias_grad_ref, x_ref, gain_ref, shift_ref, k1_ref, k2_ref, pieces_ref,
    align_ref, pack_ref, w_ref, sem,
):
    load = pltpu.make_async_copy(w_hbm, w_ref, sem)
    load.start()
    total = jnp.sum(pieces_ref[...].astype(F32).reshape(NZ, I, C * S), axis=0)
    high, low = split(total)
    scatter = one_hot(iota((S * I, I), 0) % I == iota((S * I, I), 1))
    keep = iota((S * I, C * S), 0) // I == iota((S * I, C * S), 1) % S
    fold = one_hot(iota((C * S, C), 0) // S == iota((C * S, C), 1))
    rg_high, rg_low = [
        dot(jnp.where(keep, dot(scatter, part), 0.0).astype(BF16), fold) for part in (high, low)
    ]
    right_grad = rg_high + rg_low
    high, low = split(left_grad_ref[...])
    order = to_residue_major()
    left_grad = dot(order, high, TN) + dot(order, low, TN)
    lg_high, lg_low = split(left_grad)
    rg_high, rg_low = rg_high.astype(BF16), rg_low.astype(BF16)
    normed_grad = (
        dot(lg_high, k1_ref[...])
        + dot(lg_low, k1_ref[...])
        + dot(rg_high, k2_ref[...])
        + dot(rg_low, k2_ref[...])
    )
    centred, inverse = layer_norm_parts(x_ref)
    unit = centred * inverse
    normed = (unit * gain_ref[...] + shift_ref[...]).astype(BF16)
    unit_grad = normed_grad * gain_ref[...]
    mean_one = jnp.mean(unit_grad, axis=-1, keepdims=True)
    mean_two = jnp.mean(unit_grad * unit, axis=-1, keepdims=True)
    align_ref[...] = inverse * (unit_grad - mean_one - unit * mean_two)
    gain_grad = jnp.sum(normed_grad * unit, axis=0, keepdims=True)
    offset_grad = jnp.sum(normed_grad, axis=0, keepdims=True)
    both = jnp.concatenate([lg_high, rg_high, lg_low, rg_low], axis=1)
    weights = dot(both, normed, TN)
    weights = weights[: 2 * C] + weights[2 * C :]
    weights = jnp.concatenate([weights[:, :Z], weights[:, Z:]], axis=0)
    biases = jnp.sum(jnp.concatenate([left_grad, right_grad], axis=1), axis=0, keepdims=True)
    biases = jnp.concatenate([biases, jnp.zeros((1, Z - 2 * C), F32)], axis=1)
    halves = (gain_grad[:, :Z], gain_grad[:, Z:], offset_grad[:, :Z], offset_grad[:, Z:])
    rest = jnp.concatenate(halves + (biases, bias_grad_ref[...], jnp.zeros((2, Z), F32)), axis=0)
    rest = jnp.where(iota((NP, 8, Z), 0) == 0, rest[None], 0.0)
    small = jnp.concatenate([weights.reshape(NP, 8, Z), rest], axis=1)
    load.wait()
    pack_ref[...] = packed(w_ref[...].astype(F32).reshape(NP, WR, Z), small)


def packed(w_rows, small):
    high = small.astype(BF16).astype(F32)
    return jnp.concatenate([w_rows, high, small - high], axis=1).astype(BF16)


def sum_kernel(in_ref, out_ref):
    total = jnp.sum(in_ref[...].astype(F32), axis=0)
    block = packed(total[None, :WR], total[None, WR : WR + 16] + total[None, WR + 16 :])
    out_ref[...] = jnp.broadcast_to(block, out_ref.shape)


def last_kernel(
    in_ref, gain_ref, offset_ref, lw_ref, lb_ref, rw_ref, rb_ref, w_ref, wb_ref, w_scratch
):
    blocks = in_ref[...].astype(F32)
    w_scratch[...] = blocks[:, :WR].reshape(C * C, Z)
    for c in range(C):
        w_ref[c * C : (c + 1) * C, :] = w_scratch[pl.ds(c, C, stride=C), :]
    small = blocks[:, WR : WR + 16] + blocks[:, WR + 16 :]
    weights = small[:, :8].reshape(Z, Z)
    rest = small[0, 8:]
    lw_ref[:, :Z] = weights[:C]
    lw_ref[:, Z:] = weights[2 * C : 3 * C]
    rw_ref[:, :Z] = weights[C : 2 * C]
    rw_ref[:, Z:] = weights[3 * C :]
    gain_ref[:, :Z] = rest[0:1]
    gain_ref[:, Z:] = rest[1:2]
    offset_ref[:, :Z] = rest[2:3]
    offset_ref[:, Z:] = rest[3:4]
    lb_ref[...] = rest[4:5, :C]
    rb_ref[...] = rest[4:5, C : 2 * C]
    wb_ref[...] = rest[5:6] * ROOT


def shape(dims, dtype):
    return jax.ShapeDtypeStruct(dims, dtype)


LATE = pl.CostEstimate(flops=100_000_000_000, bytes_accessed=0, transcendentals=0)
HBM = pl.BlockSpec(memory_space=pltpu.HBM)
VMEM = pl.BlockSpec(memory_space=pltpu.VMEM)


def in_hbm(array):
    return pltpu.with_memory_space_constraint(array, pltpu.HBM)


def in_vmem(*arrays):
    return [pltpu.with_memory_space_constraint(v, pltpu.VMEM) for v in arrays]


def ring(step, long):
    def number(x, z, y, core):
        return ((x % NX * NZ + z) * NY + y % NY) * 2 + core

    pairs = []
    for x, z, y, core in itertools.product(range(NX), range(NZ), range(NY), range(2)):
        by_x = long == (core == 0)
        target = number(x + step * by_x, z, y + step * (not by_x), core)
        pairs.append((number(x, z, y, core), target))
    return pairs


def shifted(arrays, long):
    return [arrays[0]] + [
        lax.ppermute(arrays[k], ("x", "z", "y", "dp"), ring(k, long)) for k in (1, 2, 3)
    ]


def call(body, name, mib, out_shape, scratch=(), **more):
    params = pltpu.CompilerParams(vmem_limit_bytes=mib * MIB)
    return pl.pallas_call(
        body, out_shape=out_shape, scratch_shapes=list(scratch), compiler_params=params, name=name, **more
    )


def exchange(array, axes):
    return lax.all_to_all(array, axes, 0, 0, tiled=True)


def blocking_exchange(array, axes):
    return lax.cond(lax.axis_index("x") < NX, lambda v: exchange(v, axes), jnp.zeros_like, array)


def per_device(x, gain, shift, k1, b1, k2, b2, w, bias, g):
    gain, shift, b1, b2, bias = [v.reshape(1, -1) for v in (gain, shift, b1, b2, bias)]
    x, k1, k2 = x.reshape(S * I, H), k1.T, k2.T
    inputs = (x, gain, shift, k1, b1, k2, b2, w, g)
    made = (
        ((I * S, C), BF16),
        ((G, C * S), BF16),
        ((C, C * Z), BF16),
        ((C * S, I * Z), BF16),
        (g.shape, BF16),
    )
    left, copies, wd, t, ordered, p0, p1, p2, p3 = call(
        first_kernel,
        "first",
        24,
        tuple(pltpu.HBM(*v) for v in made) + (pltpu.VMEM((Q, C * S), BF16),) * NX,
        [pltpu.VMEM(v.shape, v.dtype) for v in inputs]
        + [pltpu.VMEM(*v) for v in made]
        + [pltpu.VMEM((C * C, Z), F32), pltpu.VMEM(g.shape, F32), pltpu.SemaphoreType.DMA((len(inputs),))]
        + [pltpu.SemaphoreType.DMA((len(made),))],
        in_specs=[HBM] * len(inputs),
        out_specs=[HBM] * len(made) + [VMEM] * NX,
    )(*[in_hbm(v) for v in inputs])
    quarter = ((Q, C * S), BF16)
    column = ((G, C * S), BF16)
    planes = shifted((p0, p1, p2, p3), True)
    near = blocking_exchange(copies, "z")
    lines = shifted([near] * NY, False)
    parts = call(
        fold_kernel, "fold", 8, (pltpu.VMEM(*column),) * NY, [pltpu.VMEM((Q, C * S), F32)]
    )(*in_vmem(*planes))
    sums = shifted(parts, False)
    r0 = call(arrange_kernel, "arrange", 8, pltpu.VMEM(*quarter), [pltpu.VMEM((Q, C * S), F32)])(
        *in_vmem(*lines, parts[0])
    )
    r0, r1, r2, r3 = in_vmem(*shifted([r0] * NX, True))
    own = call(add_kernel, "add", 8, shape((G, C * S), F32), cost_estimate=LATE)(*in_vmem(*sums))
    pieces = exchange(own, "z")
    left_grad, w_part, bias_grad = call(
        second_kernel,
        "second",
        16,
        (shape((I * S, C), F32), pltpu.HBM((C, C, Z), BF16), shape((1, Z), F32)),
        [pltpu.VMEM(g.shape, BF16), pltpu.VMEM(wd.shape, BF16)]
        + [pltpu.VMEM((C * S + 16, J), BF16), pltpu.VMEM((I * S, C * Z), BF16), pltpu.SemaphoreType.DMA((2,))],
        in_specs=[VMEM] * NX + [HBM] * 2 + [VMEM],
        cost_estimate=LATE,
    )(r0, r1, r2, r3, in_hbm(ordered), in_hbm(wd), left)
    align, pack = call(
        third_kernel,
        "third",
        12,
        (shape((S * I, H), F32), shape((NP, WR + 32, Z), BF16)),
        [pltpu.VMEM((C, C, Z), BF16), pltpu.SemaphoreType.DMA],
        in_specs=[VMEM, HBM] + [VMEM] * 7,
    )(left_grad, in_hbm(w_part), bias_grad, x, gain, shift, k1, k2, pieces)
    parts = exchange(pack, ("x", "y"))
    update = call(
        update_kernel,
        "update",
        20,
        pltpu.HBM((I, J, Z), BF16),
        [pltpu.VMEM(t.shape, BF16), pltpu.VMEM((I, J, Z), BF16), pltpu.VMEM((J, I * Z), F32)]
        + [pltpu.SemaphoreType.DMA, pltpu.SemaphoreType.DMA((NX,))],
        in_specs=[VMEM] * NX + [HBM] + [VMEM],
        out_specs=HBM,
    )(r0, r1, r2, r3, in_hbm(t), bias)
    plane = call(sum_kernel, "sum", 8, shape((NZ, WR + 32, Z), BF16))(parts)
    column = exchange(plane, "z")
    block = call(sum_kernel, "spread", 8, shape((NP, WR + 32, Z), BF16))(column)
    sums = exchange(block, ("x", "y"))
    gain_g, offset_g, lw, lb, rw, rb, w_g, wb = call(
        last_kernel,
        "last",
        8,
        (
            shape((1, H), F32),
            shape((1, H), F32),
            shape((C, H), F32),
            shape((1, C), F32),
            shape((C, H), F32),
            shape((1, C), F32),
            shape((C * C, Z), F32),
            shape((1, Z), F32),
        ),
        [pltpu.VMEM((C * C, Z), F32)],
    )(sums)
    return (
        update,
        align.reshape(S, I, H),
        gain_g.reshape(H),
        offset_g.reshape(H),
        lw.T,
        lb.reshape(C),
        rw.T,
        rb.reshape(C),
        w_g,
        wb.reshape(Z),
    )


def solution(mesh):
    grid = Mesh(mesh.devices.reshape(NX, NZ, NY, 2), ("x", "z", "y", "dp"))
    dap = ("x", "z", "y")
    in_specs = (P("dp", dap, None),) + (P(),) * 8 + (P(("dp",) + dap, None, None),)
    out_specs = (
        P(("dp",) + dap, None, None),
        P("dp", dap, None),
        P("dp"),
        P("dp"),
        P("dp", None),
        P("dp"),
        P("dp", None),
        P("dp"),
        P("dp", None),
        P("dp"),
    )
    return jax.shard_map(
        per_device, mesh=grid, in_specs=in_specs, out_specs=out_specs, check_vma=False
    )
```

```python
import itertools
import math

import jax
import jax.numpy as jnp
from jax import lax
from jax.experimental import pallas as pl
from jax.experimental.pallas import tpu as pltpu
from jax.sharding import Mesh, PartitionSpec as P

EPSILON = 1e-05
F32 = jnp.float32
BF16 = jnp.bfloat16
S = 32
I = 8
C = 32
H = 256
Z = 128
J = 1024
NX, NZ, NY = 4, 8, 4
NP = NX * NY
WR = C * C // NP
G = NZ * I
Q = J // NX
SCALE = 1.0 / (math.sqrt(J) * S)
ROOT = 1.0 / math.sqrt(J)
NT = (((1,), (1,)), ((), ()))
TN = (((0,), (0,)), ((), ()))
MIB = 1024 * 1024


def dot(a, b, dims=(((1,), (0,)), ((), ()))):
    return lax.dot_general(a, b, dims, preferred_element_type=F32)


def iota(shape, dim):
    return lax.broadcasted_iota(jnp.int32, shape, dim)


def one_hot(condition):
    return jnp.where(condition, 1.0, 0.0).astype(BF16)


def to_residue_major():
    row, col = iota((I * S, I * S), 0), iota((I * S, I * S), 1)
    return one_hot((row // S == col % I) & (row % S == col // I))


def split(value):
    high = value.astype(BF16)
    return high, (value - high.astype(F32)).astype(BF16)


def layer_norm_parts(x_ref):
    features = x_ref[...].astype(F32)
    average = jnp.mean(features, axis=-1, keepdims=True)
    centred = features - average
    spread = jnp.mean(centred * centred, axis=-1, keepdims=True)
    inverse = lax.rsqrt(spread + EPSILON)
    return centred, inverse


def places():
    core, x, y = lax.axis_index("dp"), lax.axis_index("x"), lax.axis_index("y")
    across = Q - I
    return x + (y - x) * core, y + (x - y) * core, Q - across * core, I + across * core


def block_rows(k, n):
    own, _, long_stride, short_stride = places()
    start = (own + NX - k) % NX * long_stride + n // NY * (NY * I) + n % NY * short_stride
    return pl.ds(pl.multiple_of(start, I), I)


def copies_between(sources, targets, sems):
    return [pltpu.make_async_copy(a, b, sems.at[n]) for n, (a, b) in enumerate(zip(sources, targets))]


def first_kernel(*refs):
    inputs, outputs, held, (made, w_scratch, g_scratch, in_sems, out_sems) = (
        refs[:9], refs[9:18], refs[18:27], (refs[27:32], *refs[32:])
    )
    x_ref, gain_ref, shift_ref, k1_ref, b1_ref, k2_ref, b2_ref, w_ref, g_ref = held
    left_ref, copies_ref, wd_ref, t_ref, ordered_ref = made
    partial_refs = outputs[5:]
    loads = copies_between(inputs, held, in_sems)
    stores = copies_between(made, outputs, out_sems)
    for load in loads:
        load.start()
    for load in loads[:7]:
        load.wait()
    centred, inverse = layer_norm_parts(x_ref)
    normed = (centred * inverse * gain_ref[...] + shift_ref[...]).astype(BF16)
    left = (dot(normed, k1_ref[...], NT) + b1_ref[...]).astype(BF16)
    right = (dot(normed, k2_ref[...], NT) + b2_ref[...]).astype(BF16)
    left = dot(to_residue_major(), left).astype(BF16)
    left_ref[...] = left
    stores[0].start()
    spread = dot(right, one_hot(iota((C, C * S), 0) == iota((C, C * S), 1) // S))
    keep = iota((S * I, C * S), 0) // I == iota((S * I, C * S), 1) % S
    kept = jnp.where(keep, spread, 0.0).astype(BF16)
    gather = one_hot(iota((G, S * I), 0) % I == iota((G, S * I), 1) % I)
    copies_ref[...] = dot(gather, kept).astype(BF16)
    stores[1].start()
    loads[7].wait()
    w_scratch[...] = w_ref[...].astype(F32)
    for d in range(C):
        wd_ref[:, d * Z : (d + 1) * Z] = w_scratch[pl.ds(d, C, stride=C), :].astype(BF16)
    stores[2].start()
    for d in range(0, C, 2):
        block = dot(left, wd_ref[:, d * Z : (d + 2) * Z]).astype(BF16)
        for e in range(2):
            for i in range(I):
                t_ref[(d + e) * S : (d + e + 1) * S, i * Z : (i + 1) * Z] = block[
                    i * S : (i + 1) * S, e * Z : (e + 1) * Z
                ]
    stores[3].start()
    loads[8].wait()
    g_scratch[...] = g_ref[...].astype(F32)
    for k in range(NX):
        for n in range(0, NZ * NY, 2):
            pair = [g_scratch[:, block_rows(k, m), :] for m in (n, n + 1)]
            start = k * Q + n * I
            ordered_ref[:, start : start + 2 * I, :] = jnp.concatenate(pair, axis=1).astype(BF16)
    stores[4].start()
    rows = jnp.concatenate([ordered_ref[i] for i in range(I)], axis=1)
    whole = dot(rows, t_ref[...], NT) * SCALE
    for k in range(NX):
        start = (NX - k) % NX * Q
        partial_refs[k][...] = whole[start : start + Q].astype(BF16)
    for store in stores:
        store.wait()


def added(refs, rows):
    a, b, c, d = [ref[rows, :].astype(F32) for ref in refs]
    return (a + b) + (c + d)


def fold_kernel(*refs):
    inputs, outputs, total = refs[:4], refs[4:8], refs[8]
    line = places()[1]
    for n in range(0, Q, 16):
        rows = pl.ds(n, 16)
        total[rows, :] = added(inputs, rows)
    for k, out in enumerate(outputs):
        first = (line + k) % NY * I
        for z in range(0, NZ, 2):
            pair = [total[pl.ds(pl.multiple_of(n * NY * I + first, I), I), :] for n in (z, z + 1)]
            out[z * I : (z + 2) * I, :] = jnp.concatenate(pair, axis=0).astype(BF16)


def add_kernel(*refs):
    for n in range(0, G, 16):
        rows = pl.ds(n, 16)
        refs[4][rows, :] = added(refs[:4], rows)


def arrange_kernel(*refs):
    inputs, out_ref, total = refs[:4], refs[5], refs[6]
    line = places()[1]
    for k, ref in enumerate(inputs):
        first = (line + NY - k) % NY * I
        for z in range(0, NZ, 2):
            rows = ref[z * I : (z + 2) * I, :].astype(F32)
            for e in range(2):
                start = pl.multiple_of((z + e) * NY * I + first, I)
                total[pl.ds(start, I), :] = rows[e * I : (e + 1) * I]
    for n in range(0, Q, 16):
        out_ref[pl.ds(n, 16), :] = total[pl.ds(n, 16), :].astype(BF16)


def update_kernel(
    r0_ref, r1_ref, r2_ref, r3_ref, t_hbm, bias_ref, update_hbm, t_ref, update_ref, scratch, sem, sems
):
    load = pltpu.make_async_copy(t_hbm, t_ref, sem)
    load.start()
    load.wait()
    bias = jnp.concatenate([bias_ref[...]] * I, axis=1)
    for k, right in enumerate((r0_ref, r1_ref, r2_ref, r3_ref)):
        block = dot(right[...], t_ref[...]) * (1.0 / S) + bias
        for n in range(NZ * NY):
            scratch[block_rows(k, n), :] = block[n * I : (n + 1) * I]
    stores = []
    for k in range(NX):
        rows = pl.ds(k * Q, Q)
        for i in range(I):
            update_ref[i, rows, :] = scratch[rows, i * Z : (i + 1) * Z].astype(BF16)
        stores.append(pltpu.make_async_copy(update_ref.at[:, rows, :], update_hbm.at[:, rows, :], sems.at[k]))
        stores[-1].start()
    for store in stores:
        store.wait()


HALF = J // 2
EARLY, LATER = (0, 3), (1, 2)


def half_product(quarters, rights, g_hbm, g_ref, rt_scratch, sems, finish):
    loads = [
        pltpu.make_async_copy(
            g_hbm.at[:, pl.ds(k * Q, Q), :], g_ref.at[:, pl.ds(n * Q, Q), :], sems.at[n]
        )
        for n, k in enumerate(quarters)
    ]
    for load in loads:
        load.start()
    for k, right in enumerate(rights):
        rt_scratch[: C * S, k * Q : (k + 1) * Q] = right[...].T
    rt_scratch[C * S :, :] = jnp.ones((16, HALF), BF16)
    for load in loads:
        load.wait()
    for i in range(0, I, 2):
        finish(i, dot(rt_scratch[...], jnp.concatenate([g_ref[i], g_ref[i + 1]], axis=1)))


def early_kernel(r0_ref, re_ref, g_hbm, u_ref, g_ref, rt_scratch, sem):
    def finish(i, u):
        u_ref[:, i * Z : (i + 2) * Z] = u

    half_product(EARLY, (r0_ref, re_ref), g_hbm, g_ref, rt_scratch, sem, finish)


def second_kernel(
    ra_ref, rb_ref, u_ref, g_hbm, wd_hbm, left_ref,
    left_grad_ref, w_part_ref, bias_grad_ref,
    g_ref, wd_ref, rt_scratch, m_scratch, sem, wd_sem,
):
    load = pltpu.make_async_copy(wd_hbm, wd_ref, wd_sem)
    load.start()
    bias_grad = []

    def finish(i, u):
        u = u + u_ref[:, i * Z : (i + 2) * Z]
        bias_grad.append(u[C * S : C * S + 1, :Z] + u[C * S : C * S + 1, Z:])
        u = u[: C * S].astype(BF16)
        for e in range(2):
            for d in range(C):
                m_scratch[(i + e) * S : (i + e + 1) * S, d * Z : (d + 1) * Z] = u[
                    d * S : (d + 1) * S, e * Z : (e + 1) * Z
                ]

    half_product(LATER, (ra_ref, rb_ref), g_hbm, g_ref, rt_scratch, sem, finish)
    bias_grad = sum(bias_grad)
    bias_grad_ref[...] = bias_grad
    load.wait()
    left_grad_ref[...] = dot(m_scratch[...], wd_ref[...], NT) * SCALE
    w_part = dot(left_ref[...], m_scratch[...], TN) * SCALE
    for d in range(C):
        w_part_ref[d] = w_part[:, d * Z : (d + 1) * Z].astype(BF16)


def third_kernel(
    left_grad_ref, w_hbm, bias_grad_ref, x_ref, gain_ref, shift_ref, k1_ref, k2_ref, pieces_ref,
    align_ref, pack_ref, w_ref, sem,
):
    load = pltpu.make_async_copy(w_hbm, w_ref, sem)
    load.start()
    total = jnp.sum(pieces_ref[...].astype(F32).reshape(NZ, I, C * S), axis=0)
    high, low = split(total)
    scatter = one_hot(iota((S * I, I), 0) % I == iota((S * I, I), 1))
    keep = iota((S * I, C * S), 0) // I == iota((S * I, C * S), 1) % S
    fold = one_hot(iota((C * S, C), 0) // S == iota((C * S, C), 1))
    rg_high, rg_low = [
        dot(jnp.where(keep, dot(scatter, part), 0.0).astype(BF16), fold) for part in (high, low)
    ]
    right_grad = rg_high + rg_low
    high, low = split(left_grad_ref[...])
    order = to_residue_major()
    left_grad = dot(order, high, TN) + dot(order, low, TN)
    lg_high, lg_low = split(left_grad)
    rg_high, rg_low = rg_high.astype(BF16), rg_low.astype(BF16)
    normed_grad = (
        dot(lg_high, k1_ref[...])
        + dot(lg_low, k1_ref[...])
        + dot(rg_high, k2_ref[...])
        + dot(rg_low, k2_ref[...])
    )
    centred, inverse = layer_norm_parts(x_ref)
    unit = centred * inverse
    normed = (unit * gain_ref[...] + shift_ref[...]).astype(BF16)
    unit_grad = normed_grad * gain_ref[...]
    mean_one = jnp.mean(unit_grad, axis=-1, keepdims=True)
    mean_two = jnp.mean(unit_grad * unit, axis=-1, keepdims=True)
    align_ref[...] = inverse * (unit_grad - mean_one - unit * mean_two)
    gain_grad = jnp.sum(normed_grad * unit, axis=0, keepdims=True)
    offset_grad = jnp.sum(normed_grad, axis=0, keepdims=True)
    both = jnp.concatenate([lg_high, rg_high, lg_low, rg_low], axis=1)
    weights = dot(both, normed, TN)
    weights = weights[: 2 * C] + weights[2 * C :]
    weights = jnp.concatenate([weights[:, :Z], weights[:, Z:]], axis=0)
    biases = jnp.sum(jnp.concatenate([left_grad, right_grad], axis=1), axis=0, keepdims=True)
    biases = jnp.concatenate([biases, jnp.zeros((1, Z - 2 * C), F32)], axis=1)
    halves = (gain_grad[:, :Z], gain_grad[:, Z:], offset_grad[:, :Z], offset_grad[:, Z:])
    rest = jnp.concatenate(halves + (biases, bias_grad_ref[...], jnp.zeros((2, Z), F32)), axis=0)
    rest = jnp.where(iota((NP, 8, Z), 0) == 0, rest[None], 0.0)
    small = jnp.concatenate([weights.reshape(NP, 8, Z), rest], axis=1)
    load.wait()
    pack_ref[...] = packed(w_ref[...].astype(F32).reshape(NP, WR, Z), small)


def packed(w_rows, small):
    high = small.astype(BF16).astype(F32)
    return jnp.concatenate([w_rows, high, small - high], axis=1).astype(BF16)


def sum_kernel(in_ref, out_ref):
    total = jnp.sum(in_ref[...].astype(F32), axis=0)
    block = packed(total[None, :WR], total[None, WR : WR + 16] + total[None, WR + 16 :])
    out_ref[...] = jnp.broadcast_to(block, out_ref.shape)


def last_kernel(
    in_ref, gain_ref, offset_ref, lw_ref, lb_ref, rw_ref, rb_ref, w_ref, wb_ref, w_scratch
):
    blocks = in_ref[...].astype(F32)
    w_scratch[...] = blocks[:, :WR].reshape(C * C, Z)
    for c in range(C):
        w_ref[c * C : (c + 1) * C, :] = w_scratch[pl.ds(c, C, stride=C), :]
    small = blocks[:, WR : WR + 16] + blocks[:, WR + 16 :]
    weights = small[:, :8].reshape(Z, Z)
    rest = small[0, 8:]
    lw_ref[:, :Z] = weights[:C]
    lw_ref[:, Z:] = weights[2 * C : 3 * C]
    rw_ref[:, :Z] = weights[C : 2 * C]
    rw_ref[:, Z:] = weights[3 * C :]
    gain_ref[:, :Z] = rest[0:1]
    gain_ref[:, Z:] = rest[1:2]
    offset_ref[:, :Z] = rest[2:3]
    offset_ref[:, Z:] = rest[3:4]
    lb_ref[...] = rest[4:5, :C]
    rb_ref[...] = rest[4:5, C : 2 * C]
    wb_ref[...] = rest[5:6] * ROOT


def shape(dims, dtype):
    return jax.ShapeDtypeStruct(dims, dtype)


LATE = pl.CostEstimate(flops=100_000_000_000, bytes_accessed=0, transcendentals=0)
HBM = pl.BlockSpec(memory_space=pltpu.HBM)
VMEM = pl.BlockSpec(memory_space=pltpu.VMEM)


def in_hbm(array):
    return pltpu.with_memory_space_constraint(array, pltpu.HBM)


def in_vmem(*arrays):
    return [pltpu.with_memory_space_constraint(v, pltpu.VMEM) for v in arrays]


def ring(step, long):
    def number(x, z, y, core):
        return ((x % NX * NZ + z) * NY + y % NY) * 2 + core

    pairs = []
    for x, z, y, core in itertools.product(range(NX), range(NZ), range(NY), range(2)):
        by_x = long == (core == 0)
        target = number(x + step * by_x, z, y + step * (not by_x), core)
        pairs.append((number(x, z, y, core), target))
    return pairs


def shifted(arrays, long):
    moved = {
        k: lax.ppermute(arrays[k], ("x", "z", "y", "dp"), ring(k, long)) for k in (1, 3, 2)
    }
    return [arrays[0], moved[1], moved[2], moved[3]]


def call(body, name, mib, out_shape, scratch=(), **more):
    params = pltpu.CompilerParams(vmem_limit_bytes=mib * MIB)
    return pl.pallas_call(
        body, out_shape=out_shape, scratch_shapes=list(scratch), compiler_params=params, name=name, **more
    )


def exchange(array, axes):
    return lax.all_to_all(array, axes, 0, 0, tiled=True)


def blocking_exchange(array, axes):
    return lax.cond(lax.axis_index("x") < NX, lambda v: exchange(v, axes), jnp.zeros_like, array)


def per_device(x, gain, shift, k1, b1, k2, b2, w, bias, g):
    gain, shift, b1, b2, bias = [v.reshape(1, -1) for v in (gain, shift, b1, b2, bias)]
    x, k1, k2 = x.reshape(S * I, H), k1.T, k2.T
    inputs = (x, gain, shift, k1, b1, k2, b2, w, g)
    made = (
        ((I * S, C), BF16),
        ((G, C * S), BF16),
        ((C, C * Z), BF16),
        ((C * S, I * Z), BF16),
        (g.shape, BF16),
    )
    left, copies, wd, t, ordered, p0, p1, p2, p3 = call(
        first_kernel,
        "first",
        24,
        tuple(pltpu.HBM(*v) for v in made) + (pltpu.VMEM((Q, C * S), BF16),) * NX,
        [pltpu.VMEM(v.shape, v.dtype) for v in inputs]
        + [pltpu.VMEM(*v) for v in made]
        + [pltpu.VMEM((C * C, Z), F32), pltpu.VMEM(g.shape, F32), pltpu.SemaphoreType.DMA((len(inputs),))]
        + [pltpu.SemaphoreType.DMA((len(made),))],
        in_specs=[HBM] * len(inputs),
        out_specs=[HBM] * len(made) + [VMEM] * NX,
    )(*[in_hbm(v) for v in inputs])
    quarter = ((Q, C * S), BF16)
    column = ((G, C * S), BF16)
    planes = shifted((p0, p1, p2, p3), True)
    near = blocking_exchange(copies, "z")
    lines = shifted([near] * NY, False)
    parts = call(
        fold_kernel, "fold", 8, (pltpu.VMEM(*column),) * NY, [pltpu.VMEM((Q, C * S), F32)]
    )(*in_vmem(*planes))
    sums = shifted(parts, False)
    r0 = call(arrange_kernel, "arrange", 8, pltpu.VMEM(*quarter), [pltpu.VMEM((Q, C * S), F32)])(
        *in_vmem(*lines, parts[0])
    )
    rights = in_vmem(*shifted([r0] * NX, True))
    own = call(add_kernel, "add", 8, shape((G, C * S), F32), cost_estimate=LATE)(*in_vmem(*sums))
    pieces = exchange(own, "z")
    rt_type = ((C * S + 16, HALF), BF16)
    half = call(
        early_kernel,
        "early",
        16,
        pltpu.VMEM((C * S + 16, I * Z), F32),
        [pltpu.VMEM((I, HALF, Z), BF16), pltpu.VMEM(*rt_type), pltpu.SemaphoreType.DMA((2,))],
        in_specs=[VMEM] * 2 + [HBM],
    )(*[rights[k] for k in EARLY], in_hbm(ordered))
    left_grad, w_part, bias_grad = call(
        second_kernel,
        "second",
        16,
        (shape((I * S, C), F32), pltpu.HBM((C, C, Z), BF16), shape((1, Z), F32)),
        [pltpu.VMEM((I, HALF, Z), BF16), pltpu.VMEM(wd.shape, BF16)]
        + [pltpu.VMEM(*rt_type), pltpu.VMEM((I * S, C * Z), BF16)]
        + [pltpu.SemaphoreType.DMA((2,)), pltpu.SemaphoreType.DMA],
        in_specs=[VMEM] * 3 + [HBM] * 2 + [VMEM],
        cost_estimate=LATE,
    )(*[rights[k] for k in LATER], *in_vmem(half), in_hbm(ordered), in_hbm(wd), left)
    align, pack = call(
        third_kernel,
        "third",
        12,
        (shape((S * I, H), F32), shape((NP, WR + 32, Z), BF16)),
        [pltpu.VMEM((C, C, Z), BF16), pltpu.SemaphoreType.DMA],
        in_specs=[VMEM, HBM] + [VMEM] * 7,
    )(left_grad, in_hbm(w_part), bias_grad, x, gain, shift, k1, k2, pieces)
    parts = exchange(pack, ("x", "y"))
    update = call(
        update_kernel,
        "update",
        20,
        pltpu.HBM((I, J, Z), BF16),
        [pltpu.VMEM(t.shape, BF16), pltpu.VMEM((I, J, Z), BF16), pltpu.VMEM((J, I * Z), F32)]
        + [pltpu.SemaphoreType.DMA, pltpu.SemaphoreType.DMA((NX,))],
        in_specs=[VMEM] * NX + [HBM] + [VMEM],
        out_specs=HBM,
    )(*rights, in_hbm(t), bias)
    plane = call(sum_kernel, "sum", 8, shape((NZ, WR + 32, Z), BF16))(parts)
    column = exchange(plane, "z")
    block = call(sum_kernel, "spread", 8, shape((NP, WR + 32, Z), BF16))(column)
    sums = exchange(block, ("x", "y"))
    gain_g, offset_g, lw, lb, rw, rb, w_g, wb = call(
        last_kernel,
        "last",
        8,
        (
            shape((1, H), F32),
            shape((1, H), F32),
            shape((C, H), F32),
            shape((1, C), F32),
            shape((C, H), F32),
            shape((1, C), F32),
            shape((C * C, Z), F32),
            shape((1, Z), F32),
        ),
        [pltpu.VMEM((C * C, Z), F32)],
    )(sums)
    return (
        update,
        align.reshape(S, I, H),
        gain_g.reshape(H),
        offset_g.reshape(H),
        lw.T,
        lb.reshape(C),
        rw.T,
        rb.reshape(C),
        w_g,
        wb.reshape(Z),
    )


def solution(mesh):
    grid = Mesh(mesh.devices.reshape(NX, NZ, NY, 2), ("x", "z", "y", "dp"))
    dap = ("x", "z", "y")
    in_specs = (P("dp", dap, None),) + (P(),) * 8 + (P(("dp",) + dap, None, None),)
    out_specs = (
        P(("dp",) + dap, None, None),
        P("dp", dap, None),
        P("dp"),
        P("dp"),
        P("dp", None),
        P("dp"),
        P("dp", None),
        P("dp"),
        P("dp", None),
        P("dp"),
    )
    return jax.shard_map(
        per_device, mesh=grid, in_specs=in_specs, out_specs=out_specs, check_vma=False
    )
```

```python
import itertools
import math

import jax
import jax.numpy as jnp
from jax import lax
from jax.experimental import pallas as pl
from jax.experimental.pallas import tpu as pltpu
from jax.sharding import Mesh, PartitionSpec as P

EPSILON = 1e-05
F32 = jnp.float32
BF16 = jnp.bfloat16
S = 32
I = 8
C = 32
H = 256
Z = 128
J = 1024
NX, NZ, NY = 4, 8, 4
NP = NX * NY
WR = C * C // NP
G = NZ * I
Q = J // NX
SCALE = 1.0 / (math.sqrt(J) * S)
ROOT = 1.0 / math.sqrt(J)
NT = (((1,), (1,)), ((), ()))
TN = (((0,), (0,)), ((), ()))
MIB = 1024 * 1024


def dot(a, b, dims=(((1,), (0,)), ((), ()))):
    return lax.dot_general(a, b, dims, preferred_element_type=F32)


def iota(shape, dim):
    return lax.broadcasted_iota(jnp.int32, shape, dim)


def one_hot(condition):
    return jnp.where(condition, 1.0, 0.0).astype(BF16)


def to_residue_major():
    row, col = iota((I * S, I * S), 0), iota((I * S, I * S), 1)
    return one_hot((row // S == col % I) & (row % S == col // I))


def split(value):
    high = value.astype(BF16)
    return high, (value - high.astype(F32)).astype(BF16)


def layer_norm_parts(x_ref):
    features = x_ref[...].astype(F32)
    average = jnp.mean(features, axis=-1, keepdims=True)
    centred = features - average
    spread = jnp.mean(centred * centred, axis=-1, keepdims=True)
    inverse = lax.rsqrt(spread + EPSILON)
    return centred, inverse


def places():
    core, x, y = lax.axis_index("dp"), lax.axis_index("x"), lax.axis_index("y")
    across = Q - I
    return x + (y - x) * core, y + (x - y) * core, Q - across * core, I + across * core


def block_rows(k, n):
    own, _, long_stride, short_stride = places()
    start = (own + NX - k) % NX * long_stride + n // NY * (NY * I) + n % NY * short_stride
    return pl.ds(pl.multiple_of(start, I), I)


def copies_between(sources, targets, sems):
    return [pltpu.make_async_copy(a, b, sems.at[n]) for n, (a, b) in enumerate(zip(sources, targets))]


def first_kernel(*refs):
    inputs, outputs, held, (made, w_scratch, g_scratch, in_sems, out_sems) = (
        refs[:9], refs[9:18], refs[18:27], (refs[27:32], *refs[32:])
    )
    x_ref, gain_ref, shift_ref, k1_ref, b1_ref, k2_ref, b2_ref, w_ref, g_ref = held
    left_ref, copies_ref, wd_ref, t_ref, ordered_ref = made
    partial_refs = outputs[5:]
    loads = copies_between(inputs, held, in_sems)
    stores = copies_between(made, outputs, out_sems)
    for load in loads:
        load.start()
    for load in loads[:7]:
        load.wait()
    centred, inverse = layer_norm_parts(x_ref)
    normed = (centred * inverse * gain_ref[...] + shift_ref[...]).astype(BF16)
    left = (dot(normed, k1_ref[...], NT) + b1_ref[...]).astype(BF16)
    right = (dot(normed, k2_ref[...], NT) + b2_ref[...]).astype(BF16)
    left = dot(to_residue_major(), left).astype(BF16)
    left_ref[...] = left
    stores[0].start()
    spread = dot(right, one_hot(iota((C, C * S), 0) == iota((C, C * S), 1) // S))
    keep = iota((S * I, C * S), 0) // I == iota((S * I, C * S), 1) % S
    kept = jnp.where(keep, spread, 0.0).astype(BF16)
    gather = one_hot(iota((G, S * I), 0) % I == iota((G, S * I), 1) % I)
    copies_ref[...] = dot(gather, kept).astype(BF16)
    stores[1].start()
    loads[7].wait()
    w_scratch[...] = w_ref[...].astype(F32)
    for d in range(C):
        wd_ref[:, d * Z : (d + 1) * Z] = w_scratch[pl.ds(d, C, stride=C), :].astype(BF16)
    stores[2].start()
    for d in range(0, C, 2):
        block = dot(left, wd_ref[:, d * Z : (d + 2) * Z]).astype(BF16)
        for e in range(2):
            for i in range(I):
                t_ref[(d + e) * S : (d + e + 1) * S, i * Z : (i + 1) * Z] = block[
                    i * S : (i + 1) * S, e * Z : (e + 1) * Z
                ]
    stores[3].start()
    loads[8].wait()
    g_scratch[...] = g_ref[...].astype(F32)
    for k in range(NX):
        for n in range(0, NZ * NY, 2):
            pair = [g_scratch[:, block_rows(k, m), :] for m in (n, n + 1)]
            start = k * Q + n * I
            ordered_ref[:, start : start + 2 * I, :] = jnp.concatenate(pair, axis=1).astype(BF16)
    stores[4].start()
    rows = jnp.concatenate([ordered_ref[i] for i in range(I)], axis=1)
    whole = dot(rows, t_ref[...], NT) * SCALE
    for k in range(NX):
        start = (NX - k) % NX * Q
        partial_refs[k][...] = whole[start : start + Q].astype(BF16)
    for store in stores:
        store.wait()


def added(refs, rows):
    a, b, c, d = [ref[rows, :].astype(F32) for ref in refs]
    return (a + b) + (c + d)


def fold_kernel(*refs):
    inputs, outputs, total = refs[:4], refs[4:8], refs[8]
    line = places()[1]
    for n in range(0, Q, 16):
        rows = pl.ds(n, 16)
        total[rows, :] = added(inputs, rows)
    for k, out in enumerate(outputs):
        first = (line + k) % NY * I
        for z in range(0, NZ, 2):
            pair = [total[pl.ds(pl.multiple_of(n * NY * I + first, I), I), :] for n in (z, z + 1)]
            out[z * I : (z + 2) * I, :] = jnp.concatenate(pair, axis=0).astype(BF16)


def add_kernel(*refs):
    for n in range(0, G, 16):
        rows = pl.ds(n, 16)
        refs[4][rows, :] = added(refs[:4], rows)


def arrange_kernel(*refs):
    inputs, out_ref, total = refs[:4], refs[5], refs[6]
    line = places()[1]
    for k, ref in enumerate(inputs):
        first = (line + NY - k) % NY * I
        for z in range(0, NZ, 2):
            rows = ref[z * I : (z + 2) * I, :].astype(F32)
            for e in range(2):
                start = pl.multiple_of((z + e) * NY * I + first, I)
                total[pl.ds(start, I), :] = rows[e * I : (e + 1) * I]
    for n in range(0, Q, 16):
        out_ref[pl.ds(n, 16), :] = total[pl.ds(n, 16), :].astype(BF16)


def update_kernel(
    r0_ref, r1_ref, r2_ref, r3_ref, t_hbm, bias_ref, update_hbm, t_ref, update_ref, scratch, sem, sems
):
    load = pltpu.make_async_copy(t_hbm, t_ref, sem)
    load.start()
    load.wait()
    bias = jnp.concatenate([bias_ref[...]] * I, axis=1)
    for k, right in enumerate((r0_ref, r1_ref, r2_ref, r3_ref)):
        block = dot(right[...], t_ref[...]) * (1.0 / S) + bias
        for n in range(NZ * NY):
            scratch[block_rows(k, n), :] = block[n * I : (n + 1) * I]
    stores = []
    for k in range(NX):
        rows = pl.ds(k * Q, Q)
        for i in range(I):
            update_ref[i, rows, :] = scratch[rows, i * Z : (i + 1) * Z].astype(BF16)
        stores.append(pltpu.make_async_copy(update_ref.at[:, rows, :], update_hbm.at[:, rows, :], sems.at[k]))
        stores[-1].start()
    for store in stores:
        store.wait()


HALF = J // 2
EARLY, LATER = (0, 3), (1, 2)


def half_product(quarters, rights, g_hbm, g_ref, rt_scratch, sems, finish):
    loads = [
        pltpu.make_async_copy(
            g_hbm.at[:, pl.ds(k * Q, Q), :], g_ref.at[:, pl.ds(n * Q, Q), :], sems.at[n]
        )
        for n, k in enumerate(quarters)
    ]
    for load in loads:
        load.start()
    for k, right in enumerate(rights):
        rt_scratch[: C * S, k * Q : (k + 1) * Q] = right[...].T
    rt_scratch[C * S :, :] = jnp.ones((16, HALF), BF16)
    for load in loads:
        load.wait()
    for i in range(0, I, 2):
        finish(i, dot(rt_scratch[...], jnp.concatenate([g_ref[i], g_ref[i + 1]], axis=1)))


def early_kernel(r0_ref, re_ref, g_hbm, u_ref, g_ref, rt_scratch, sem):
    def finish(i, u):
        u_ref[:, i * Z : (i + 2) * Z] = u

    half_product(EARLY, (r0_ref, re_ref), g_hbm, g_ref, rt_scratch, sem, finish)


def second_kernel(
    ra_ref, rb_ref, u_ref, g_hbm, wd_hbm, left_ref,
    left_grad_ref, w_part_hbm, bias_grad_ref,
    g_ref, wd_ref, w_part_ref, rt_scratch, m_scratch, sem, wd_sem, w_sem,
):
    load = pltpu.make_async_copy(wd_hbm, wd_ref, wd_sem)
    load.start()
    bias_grad = []

    def finish(i, u):
        u = u + u_ref[:, i * Z : (i + 2) * Z]
        bias_grad.append(u[C * S : C * S + 1, :Z] + u[C * S : C * S + 1, Z:])
        u = u[: C * S].astype(BF16)
        for e in range(2):
            for d in range(C):
                m_scratch[(i + e) * S : (i + e + 1) * S, d * Z : (d + 1) * Z] = u[
                    d * S : (d + 1) * S, e * Z : (e + 1) * Z
                ]

    half_product(LATER, (ra_ref, rb_ref), g_hbm, g_ref, rt_scratch, sem, finish)
    bias_grad = sum(bias_grad)
    bias_grad_ref[...] = bias_grad
    w_part = dot(left_ref[...], m_scratch[...], TN) * SCALE
    for d in range(C):
        w_part_ref[d] = w_part[:, d * Z : (d + 1) * Z].astype(BF16)
    store = pltpu.make_async_copy(w_part_ref, w_part_hbm, w_sem)
    store.start()
    load.wait()
    left_grad_ref[...] = dot(m_scratch[...], wd_ref[...], NT) * SCALE
    store.wait()


def third_kernel(
    left_grad_ref, w_hbm, bias_grad_ref, x_ref, gain_ref, shift_ref, k1_ref, k2_ref, pieces_ref,
    align_hbm, pack_ref, w_ref, align_ref, sem, align_sem,
):
    load = pltpu.make_async_copy(w_hbm, w_ref, sem)
    load.start()
    total = jnp.sum(pieces_ref[...].astype(F32).reshape(NZ, I, C * S), axis=0)
    high, low = split(total)
    scatter = one_hot(iota((S * I, I), 0) % I == iota((S * I, I), 1))
    keep = iota((S * I, C * S), 0) // I == iota((S * I, C * S), 1) % S
    fold = one_hot(iota((C * S, C), 0) // S == iota((C * S, C), 1))
    rg_high, rg_low = [
        dot(jnp.where(keep, dot(scatter, part), 0.0).astype(BF16), fold) for part in (high, low)
    ]
    right_grad = rg_high + rg_low
    high, low = split(left_grad_ref[...])
    order = to_residue_major()
    left_grad = dot(order, high, TN) + dot(order, low, TN)
    lg_high, lg_low = split(left_grad)
    rg_high, rg_low = rg_high.astype(BF16), rg_low.astype(BF16)
    normed_grad = (
        dot(lg_high, k1_ref[...])
        + dot(lg_low, k1_ref[...])
        + dot(rg_high, k2_ref[...])
        + dot(rg_low, k2_ref[...])
    )
    centred, inverse = layer_norm_parts(x_ref)
    unit = centred * inverse
    normed = (unit * gain_ref[...] + shift_ref[...]).astype(BF16)
    unit_grad = normed_grad * gain_ref[...]
    mean_one = jnp.mean(unit_grad, axis=-1, keepdims=True)
    mean_two = jnp.mean(unit_grad * unit, axis=-1, keepdims=True)
    align_ref[...] = inverse * (unit_grad - mean_one - unit * mean_two)
    store = pltpu.make_async_copy(align_ref, align_hbm, align_sem)
    store.start()
    gain_grad = jnp.sum(normed_grad * unit, axis=0, keepdims=True)
    offset_grad = jnp.sum(normed_grad, axis=0, keepdims=True)
    both = jnp.concatenate([lg_high, rg_high, lg_low, rg_low], axis=1)
    weights = dot(both, normed, TN)
    weights = weights[: 2 * C] + weights[2 * C :]
    weights = jnp.concatenate([weights[:, :Z], weights[:, Z:]], axis=0)
    biases = jnp.sum(jnp.concatenate([left_grad, right_grad], axis=1), axis=0, keepdims=True)
    biases = jnp.concatenate([biases, jnp.zeros((1, Z - 2 * C), F32)], axis=1)
    halves = (gain_grad[:, :Z], gain_grad[:, Z:], offset_grad[:, :Z], offset_grad[:, Z:])
    rest = jnp.concatenate(halves + (biases, bias_grad_ref[...], jnp.zeros((2, Z), F32)), axis=0)
    rest = jnp.where(iota((NP, 8, Z), 0) == 0, rest[None], 0.0)
    small = jnp.concatenate([weights.reshape(NP, 8, Z), rest], axis=1)
    load.wait()
    pack_ref[...] = packed(w_ref[...].astype(F32).reshape(NP, WR, Z), small)
    store.wait()


def packed(w_rows, small):
    high = small.astype(BF16).astype(F32)
    return jnp.concatenate([w_rows, high, small - high], axis=1).astype(BF16)


def sum_kernel(in_ref, out_ref):
    total = jnp.sum(in_ref[...].astype(F32), axis=0)
    block = packed(total[None, :WR], total[None, WR : WR + 16] + total[None, WR + 16 :])
    out_ref[...] = jnp.broadcast_to(block, out_ref.shape)


def last_kernel(
    in_ref, gain_ref, offset_ref, lw_ref, lb_ref, rw_ref, rb_ref, w_ref, wb_ref, w_scratch
):
    blocks = in_ref[...].astype(F32)
    w_scratch[...] = blocks[:, :WR].reshape(C * C, Z)
    for c in range(C):
        w_ref[c * C : (c + 1) * C, :] = w_scratch[pl.ds(c, C, stride=C), :]
    small = blocks[:, WR : WR + 16] + blocks[:, WR + 16 :]
    weights = small[:, :8].reshape(Z, Z)
    rest = small[0, 8:]
    lw_ref[:, :Z] = weights[:C]
    lw_ref[:, Z:] = weights[2 * C : 3 * C]
    rw_ref[:, :Z] = weights[C : 2 * C]
    rw_ref[:, Z:] = weights[3 * C :]
    gain_ref[:, :Z] = rest[0:1]
    gain_ref[:, Z:] = rest[1:2]
    offset_ref[:, :Z] = rest[2:3]
    offset_ref[:, Z:] = rest[3:4]
    lb_ref[...] = rest[4:5, :C]
    rb_ref[...] = rest[4:5, C : 2 * C]
    wb_ref[...] = rest[5:6] * ROOT


def shape(dims, dtype):
    return jax.ShapeDtypeStruct(dims, dtype)


LATE = pl.CostEstimate(flops=100_000_000_000, bytes_accessed=0, transcendentals=0)
HBM = pl.BlockSpec(memory_space=pltpu.HBM)
VMEM = pl.BlockSpec(memory_space=pltpu.VMEM)


def in_hbm(array):
    return pltpu.with_memory_space_constraint(array, pltpu.HBM)


def in_vmem(*arrays):
    return [pltpu.with_memory_space_constraint(v, pltpu.VMEM) for v in arrays]


def ring(step, long):
    def number(x, z, y, core):
        return ((x % NX * NZ + z) * NY + y % NY) * 2 + core

    pairs = []
    for x, z, y, core in itertools.product(range(NX), range(NZ), range(NY), range(2)):
        by_x = long == (core == 0)
        target = number(x + step * by_x, z, y + step * (not by_x), core)
        pairs.append((number(x, z, y, core), target))
    return pairs


def shifted(arrays, long):
    moved = {
        k: lax.ppermute(arrays[k], ("x", "z", "y", "dp"), ring(k, long)) for k in (1, 3, 2)
    }
    return [arrays[0], moved[1], moved[2], moved[3]]


def call(body, name, mib, out_shape, scratch=(), **more):
    params = pltpu.CompilerParams(vmem_limit_bytes=mib * MIB)
    return pl.pallas_call(
        body, out_shape=out_shape, scratch_shapes=list(scratch), compiler_params=params, name=name, **more
    )


def exchange(array, axes):
    return lax.all_to_all(array, axes, 0, 0, tiled=True)


def per_device(x, gain, shift, k1, b1, k2, b2, w, bias, g):
    gain, shift, b1, b2, bias = [v.reshape(1, -1) for v in (gain, shift, b1, b2, bias)]
    x, k1, k2 = x.reshape(S * I, H), k1.T, k2.T
    inputs = (x, gain, shift, k1, b1, k2, b2, w, g)
    made = (
        ((I * S, C), BF16),
        ((G, C * S), BF16),
        ((C, C * Z), BF16),
        ((C * S, I * Z), BF16),
        (g.shape, BF16),
    )
    left, copies, wd, t, ordered, p0, p1, p2, p3 = call(
        first_kernel,
        "first",
        24,
        tuple(pltpu.HBM(*v) for v in made) + (pltpu.VMEM((Q, C * S), BF16),) * NX,
        [pltpu.VMEM(v.shape, v.dtype) for v in inputs]
        + [pltpu.VMEM(*v) for v in made]
        + [pltpu.VMEM((C * C, Z), F32), pltpu.VMEM(g.shape, F32), pltpu.SemaphoreType.DMA((len(inputs),))]
        + [pltpu.SemaphoreType.DMA((len(made),))],
        in_specs=[HBM] * len(inputs),
        out_specs=[HBM] * len(made) + [VMEM] * NX,
    )(*[in_hbm(v) for v in inputs])
    quarter = ((Q, C * S), BF16)
    column = ((G, C * S), BF16)
    planes = shifted((p0, p1, p2, p3), True)
    near = exchange(copies, "z")
    lines = shifted([near] * NY, False)
    parts = call(
        fold_kernel, "fold", 8, (pltpu.VMEM(*column),) * NY, [pltpu.VMEM((Q, C * S), F32)]
    )(*in_vmem(*planes))
    sums = shifted(parts, False)
    r0 = call(arrange_kernel, "arrange", 8, pltpu.VMEM(*quarter), [pltpu.VMEM((Q, C * S), F32)])(
        *in_vmem(*lines, parts[0])
    )
    rights = in_vmem(*shifted([r0] * NX, True))
    own = call(add_kernel, "add", 8, shape((G, C * S), F32), cost_estimate=LATE)(*in_vmem(*sums))
    pieces = exchange(own, "z")
    rt_type = ((C * S + 16, HALF), BF16)
    half = call(
        early_kernel,
        "early",
        16,
        pltpu.VMEM((C * S + 16, I * Z), F32),
        [pltpu.VMEM((I, HALF, Z), BF16), pltpu.VMEM(*rt_type), pltpu.SemaphoreType.DMA((2,))],
        in_specs=[VMEM] * 2 + [HBM],
    )(*[rights[k] for k in EARLY], in_hbm(ordered))
    left_grad, w_part, bias_grad = call(
        second_kernel,
        "second",
        16,
        (shape((I * S, C), F32), pltpu.HBM((C, C, Z), BF16), shape((1, Z), F32)),
        [pltpu.VMEM((I, HALF, Z), BF16), pltpu.VMEM(wd.shape, BF16), pltpu.VMEM((C, C, Z), BF16)]
        + [pltpu.VMEM(*rt_type), pltpu.VMEM((I * S, C * Z), BF16)]
        + [pltpu.SemaphoreType.DMA((2,)), pltpu.SemaphoreType.DMA, pltpu.SemaphoreType.DMA],
        in_specs=[VMEM] * 3 + [HBM] * 2 + [VMEM],
        out_specs=[VMEM, HBM, VMEM],
        cost_estimate=LATE,
    )(*[rights[k] for k in LATER], *in_vmem(half), in_hbm(ordered), in_hbm(wd), left)
    align, pack = call(
        third_kernel,
        "third",
        12,
        (pltpu.HBM((S * I, H), F32), shape((NP, WR + 32, Z), BF16)),
        [pltpu.VMEM((C, C, Z), BF16), pltpu.VMEM((S * I, H), F32)]
        + [pltpu.SemaphoreType.DMA, pltpu.SemaphoreType.DMA],
        out_specs=[HBM, VMEM],
        in_specs=[VMEM, HBM] + [VMEM] * 7,
    )(left_grad, in_hbm(w_part), bias_grad, x, gain, shift, k1, k2, pieces)
    parts = exchange(pack, ("x", "y"))
    update = call(
        update_kernel,
        "update",
        20,
        pltpu.HBM((I, J, Z), BF16),
        [pltpu.VMEM(t.shape, BF16), pltpu.VMEM((I, J, Z), BF16), pltpu.VMEM((J, I * Z), F32)]
        + [pltpu.SemaphoreType.DMA, pltpu.SemaphoreType.DMA((NX,))],
        in_specs=[VMEM] * NX + [HBM] + [VMEM],
        out_specs=HBM,
    )(*rights, in_hbm(t), bias)
    plane = call(sum_kernel, "sum", 8, shape((NZ, WR + 32, Z), BF16))(parts)
    column = exchange(plane, "z")
    block = call(sum_kernel, "spread", 8, shape((NP, WR + 32, Z), BF16))(column)
    sums = exchange(block, ("x", "y"))
    gain_g, offset_g, lw, lb, rw, rb, w_g, wb = call(
        last_kernel,
        "last",
        8,
        (
            shape((1, H), F32),
            shape((1, H), F32),
            shape((C, H), F32),
            shape((1, C), F32),
            shape((C, H), F32),
            shape((1, C), F32),
            shape((C * C, Z), F32),
            shape((1, Z), F32),
        ),
        [pltpu.VMEM((C * C, Z), F32)],
    )(sums)
    return (
        update,
        align.reshape(S, I, H),
        gain_g.reshape(H),
        offset_g.reshape(H),
        lw.T,
        lb.reshape(C),
        rw.T,
        rb.reshape(C),
        w_g,
        wb.reshape(Z),
    )


def solution(mesh):
    grid = Mesh(mesh.devices.reshape(NX, NZ, NY, 2), ("x", "z", "y", "dp"))
    dap = ("x", "z", "y")
    in_specs = (P("dp", dap, None),) + (P(),) * 8 + (P(("dp",) + dap, None, None),)
    out_specs = (
        P(("dp",) + dap, None, None),
        P("dp", dap, None),
        P("dp"),
        P("dp"),
        P("dp", None),
        P("dp"),
        P("dp", None),
        P("dp"),
        P("dp", None),
        P("dp"),
    )
    return jax.shard_map(
        per_device, mesh=grid, in_specs=in_specs, out_specs=out_specs, check_vma=False
    )
```

```python
import itertools
import math

import jax
import jax.numpy as jnp
from jax import lax
from jax.experimental import pallas as pl
from jax.experimental.pallas import tpu as pltpu
from jax.sharding import Mesh, PartitionSpec as P

EPSILON = 1e-05
F32 = jnp.float32
BF16 = jnp.bfloat16
S = 32
I = 8
C = 32
H = 256
Z = 128
J = 1024
NX, NZ, NY = 4, 8, 4
NP = NX * NY
WR = C * C // NP
G = NZ * I
Q = J // NX
SCALE = 1.0 / (math.sqrt(J) * S)
ROOT = 1.0 / math.sqrt(J)
NT = (((1,), (1,)), ((), ()))
TN = (((0,), (0,)), ((), ()))
MIB = 1024 * 1024


def dot(a, b, dims=(((1,), (0,)), ((), ()))):
    return lax.dot_general(a, b, dims, preferred_element_type=F32)


def iota(shape, dim):
    return lax.broadcasted_iota(jnp.int32, shape, dim)


def one_hot(condition):
    return jnp.where(condition, 1.0, 0.0).astype(BF16)


def to_residue_major():
    row, col = iota((I * S, I * S), 0), iota((I * S, I * S), 1)
    return one_hot((row // S == col % I) & (row % S == col // I))


def split(value):
    high = value.astype(BF16)
    return high, (value - high.astype(F32)).astype(BF16)


def layer_norm_parts(x_ref):
    features = x_ref[...].astype(F32)
    average = jnp.mean(features, axis=-1, keepdims=True)
    centred = features - average
    spread = jnp.mean(centred * centred, axis=-1, keepdims=True)
    inverse = lax.rsqrt(spread + EPSILON)
    return centred, inverse


def places():
    core, x, y = lax.axis_index("dp"), lax.axis_index("x"), lax.axis_index("y")
    across = Q - I
    return x + (y - x) * core, y + (x - y) * core, Q - across * core, I + across * core


def block_rows(k, n):
    own, _, long_stride, short_stride = places()
    start = (own + NX - k) % NX * long_stride + n // NY * (NY * I) + n % NY * short_stride
    return pl.ds(pl.multiple_of(start, I), I)


def copies_between(sources, targets, sems):
    return [pltpu.make_async_copy(a, b, sems.at[n]) for n, (a, b) in enumerate(zip(sources, targets))]


def first_kernel(*refs):
    inputs, outputs, held, (made, w_scratch, g_scratch, in_sems, out_sems) = (
        refs[:9], refs[9:18], refs[18:27], (refs[27:32], *refs[32:])
    )
    x_ref, gain_ref, shift_ref, k1_ref, b1_ref, k2_ref, b2_ref, w_ref, g_ref = held
    left_ref, copies_ref, wd_ref, t_ref, ordered_ref = made
    partial_refs = outputs[5:]
    loads = copies_between(inputs, held, in_sems)
    stores = copies_between(made, outputs, out_sems)
    for load in loads:
        load.start()
    for load in loads[:7]:
        load.wait()
    centred, inverse = layer_norm_parts(x_ref)
    normed = (centred * inverse * gain_ref[...] + shift_ref[...]).astype(BF16)
    left = (dot(normed, k1_ref[...], NT) + b1_ref[...]).astype(BF16)
    right = (dot(normed, k2_ref[...], NT) + b2_ref[...]).astype(BF16)
    left = dot(to_residue_major(), left).astype(BF16)
    left_ref[...] = left
    stores[0].start()
    spread = dot(right, one_hot(iota((C, C * S), 0) == iota((C, C * S), 1) // S))
    keep = iota((S * I, C * S), 0) // I == iota((S * I, C * S), 1) % S
    kept = jnp.where(keep, spread, 0.0).astype(BF16)
    gather = one_hot(iota((G, S * I), 0) % I == iota((G, S * I), 1) % I)
    copies_ref[...] = dot(gather, kept).astype(BF16)
    stores[1].start()
    loads[7].wait()
    w_scratch[...] = w_ref[...].astype(F32)
    for d in range(C):
        wd_ref[:, d * Z : (d + 1) * Z] = w_scratch[pl.ds(d, C, stride=C), :].astype(BF16)
    stores[2].start()
    for d in range(0, C, 2):
        block = dot(left, wd_ref[:, d * Z : (d + 2) * Z]).astype(BF16)
        for e in range(2):
            for i in range(I):
                t_ref[(d + e) * S : (d + e + 1) * S, i * Z : (i + 1) * Z] = block[
                    i * S : (i + 1) * S, e * Z : (e + 1) * Z
                ]
    stores[3].start()
    loads[8].wait()
    g_scratch[...] = g_ref[...].astype(F32)
    for k in range(NX):
        for n in range(0, NZ * NY, 2):
            pair = [g_scratch[:, block_rows(k, m), :] for m in (n, n + 1)]
            start = k * Q + n * I
            ordered_ref[:, start : start + 2 * I, :] = jnp.concatenate(pair, axis=1).astype(BF16)
    stores[4].start()
    rows = jnp.concatenate([ordered_ref[i] for i in range(I)], axis=1)
    whole = dot(rows, t_ref[...], NT) * SCALE
    for k in range(NX):
        start = (NX - k) % NX * Q
        partial_refs[k][...] = whole[start : start + Q].astype(BF16)
    for store in stores:
        store.wait()


def added(refs, rows):
    a, b, c, d = [ref[rows, :].astype(F32) for ref in refs]
    return (a + b) + (c + d)


def fold_kernel(*refs):
    inputs, outputs, total = refs[:4], refs[4:8], refs[8]
    line = places()[1]
    for n in range(0, Q, 16):
        rows = pl.ds(n, 16)
        total[rows, :] = added(inputs, rows)
    for k, out in enumerate(outputs):
        first = (line + k) % NY * I
        for z in range(0, NZ, 2):
            pair = [total[pl.ds(pl.multiple_of(n * NY * I + first, I), I), :] for n in (z, z + 1)]
            out[z * I : (z + 2) * I, :] = jnp.concatenate(pair, axis=0).astype(BF16)


def add_kernel(*refs):
    for n in range(0, G, 16):
        rows = pl.ds(n, 16)
        refs[4][rows, :] = added(refs[:4], rows)


def arrange_kernel(*refs):
    inputs, out_ref, total = refs[:4], refs[5], refs[6]
    line = places()[1]
    for k, ref in enumerate(inputs):
        first = (line + NY - k) % NY * I
        for z in range(0, NZ, 2):
            rows = ref[z * I : (z + 2) * I, :].astype(F32)
            for e in range(2):
                start = pl.multiple_of((z + e) * NY * I + first, I)
                total[pl.ds(start, I), :] = rows[e * I : (e + 1) * I]
    for n in range(0, Q, 16):
        out_ref[pl.ds(n, 16), :] = total[pl.ds(n, 16), :].astype(BF16)


def update_kernel(
    r0_ref, r1_ref, r2_ref, r3_ref, t_hbm, bias_ref, update_hbm, t_ref, update_ref, scratch, sem, sems
):
    load = pltpu.make_async_copy(t_hbm, t_ref, sem)
    load.start()
    load.wait()
    bias = jnp.concatenate([bias_ref[...]] * I, axis=1)
    for k, right in enumerate((r0_ref, r1_ref, r2_ref, r3_ref)):
        block = dot(right[...], t_ref[...]) * (1.0 / S) + bias
        for n in range(NZ * NY):
            scratch[block_rows(k, n), :] = block[n * I : (n + 1) * I]
    stores = []
    for k in range(NX):
        rows = pl.ds(k * Q, Q)
        for i in range(I):
            update_ref[i, rows, :] = scratch[rows, i * Z : (i + 1) * Z].astype(BF16)
        stores.append(pltpu.make_async_copy(update_ref.at[:, rows, :], update_hbm.at[:, rows, :], sems.at[k]))
        stores[-1].start()
    for store in stores:
        store.wait()


HALF = J // 2
EARLY, LATER = (0, 3), (1, 2)


def half_product(quarters, rights, g_hbm, g_ref, rt_scratch, sems, finish):
    loads = [
        pltpu.make_async_copy(
            g_hbm.at[:, pl.ds(k * Q, Q), :], g_ref.at[:, pl.ds(n * Q, Q), :], sems.at[n]
        )
        for n, k in enumerate(quarters)
    ]
    for load in loads:
        load.start()
    for k, right in enumerate(rights):
        rt_scratch[: C * S, k * Q : (k + 1) * Q] = right[...].T
    rt_scratch[C * S :, :] = jnp.ones((16, HALF), BF16)
    for load in loads:
        load.wait()
    for i in range(0, I, 2):
        finish(i, dot(rt_scratch[...], jnp.concatenate([g_ref[i], g_ref[i + 1]], axis=1)))


def early_kernel(r0_ref, re_ref, g_hbm, u_ref, g_ref, rt_scratch, sem):
    def finish(i, u):
        u_ref[:, i * Z : (i + 2) * Z] = u

    half_product(EARLY, (r0_ref, re_ref), g_hbm, g_ref, rt_scratch, sem, finish)


def second_kernel(
    ra_ref, rb_ref, u_ref, g_hbm, wd_hbm, left_ref,
    left_grad_ref, w_part_ref, bias_grad_ref,
    g_ref, wd_ref, rt_scratch, m_scratch, sem, wd_sem,
):
    load = pltpu.make_async_copy(wd_hbm, wd_ref, wd_sem)
    load.start()
    bias_grad = []

    def finish(i, u):
        u = u + u_ref[:, i * Z : (i + 2) * Z]
        bias_grad.append(u[C * S : C * S + 1, :Z] + u[C * S : C * S + 1, Z:])
        u = u[: C * S].astype(BF16)
        for e in range(2):
            for d in range(C):
                m_scratch[(i + e) * S : (i + e + 1) * S, d * Z : (d + 1) * Z] = u[
                    d * S : (d + 1) * S, e * Z : (e + 1) * Z
                ]

    half_product(LATER, (ra_ref, rb_ref), g_hbm, g_ref, rt_scratch, sem, finish)
    bias_grad = sum(bias_grad)
    bias_grad_ref[...] = bias_grad
    load.wait()
    left_grad_ref[...] = dot(m_scratch[...], wd_ref[...], NT) * SCALE
    w_part = dot(left_ref[...], m_scratch[...], TN) * SCALE
    for d in range(C):
        w_part_ref[d] = w_part[:, d * Z : (d + 1) * Z].astype(BF16)


def third_kernel(
    left_grad_ref, w_hbm, bias_grad_ref, x_ref, gain_ref, shift_ref, k1_ref, k2_ref, pieces_ref,
    align_hbm, pack_ref, w_ref, align_ref, sem, align_sem,
):
    load = pltpu.make_async_copy(w_hbm, w_ref, sem)
    load.start()
    total = jnp.sum(pieces_ref[...].astype(F32).reshape(NZ, I, C * S), axis=0)
    high, low = split(total)
    scatter = one_hot(iota((S * I, I), 0) % I == iota((S * I, I), 1))
    keep = iota((S * I, C * S), 0) // I == iota((S * I, C * S), 1) % S
    fold = one_hot(iota((C * S, C), 0) // S == iota((C * S, C), 1))
    rg_high, rg_low = [
        dot(jnp.where(keep, dot(scatter, part), 0.0).astype(BF16), fold) for part in (high, low)
    ]
    right_grad = rg_high + rg_low
    high, low = split(left_grad_ref[...])
    order = to_residue_major()
    left_grad = dot(order, high, TN) + dot(order, low, TN)
    lg_high, lg_low = split(left_grad)
    rg_high, rg_low = rg_high.astype(BF16), rg_low.astype(BF16)
    normed_grad = (
        dot(lg_high, k1_ref[...])
        + dot(lg_low, k1_ref[...])
        + dot(rg_high, k2_ref[...])
        + dot(rg_low, k2_ref[...])
    )
    centred, inverse = layer_norm_parts(x_ref)
    unit = centred * inverse
    normed = (unit * gain_ref[...] + shift_ref[...]).astype(BF16)
    unit_grad = normed_grad * gain_ref[...]
    mean_one = jnp.mean(unit_grad, axis=-1, keepdims=True)
    mean_two = jnp.mean(unit_grad * unit, axis=-1, keepdims=True)
    align_ref[...] = inverse * (unit_grad - mean_one - unit * mean_two)
    store = pltpu.make_async_copy(align_ref, align_hbm, align_sem)
    store.start()
    gain_grad = jnp.sum(normed_grad * unit, axis=0, keepdims=True)
    offset_grad = jnp.sum(normed_grad, axis=0, keepdims=True)
    both = jnp.concatenate([lg_high, rg_high, lg_low, rg_low], axis=1)
    weights = dot(both, normed, TN)
    weights = weights[: 2 * C] + weights[2 * C :]
    weights = jnp.concatenate([weights[:, :Z], weights[:, Z:]], axis=0)
    biases = jnp.sum(jnp.concatenate([left_grad, right_grad], axis=1), axis=0, keepdims=True)
    biases = jnp.concatenate([biases, jnp.zeros((1, Z - 2 * C), F32)], axis=1)
    halves = (gain_grad[:, :Z], gain_grad[:, Z:], offset_grad[:, :Z], offset_grad[:, Z:])
    rest = jnp.concatenate(halves + (biases, bias_grad_ref[...], jnp.zeros((2, Z), F32)), axis=0)
    rest = jnp.where(iota((NP, 8, Z), 0) == 0, rest[None], 0.0)
    small = jnp.concatenate([weights.reshape(NP, 8, Z), rest], axis=1)
    load.wait()
    pack_ref[...] = packed(w_ref[...].astype(F32).reshape(NP, WR, Z), small)
    store.wait()


def packed(w_rows, small):
    high = small.astype(BF16).astype(F32)
    return jnp.concatenate([w_rows, high, small - high], axis=1).astype(BF16)


def sum_kernel(in_ref, out_ref):
    total = jnp.sum(in_ref[...].astype(F32), axis=0)
    block = packed(total[None, :WR], total[None, WR : WR + 16] + total[None, WR + 16 :])
    out_ref[...] = jnp.broadcast_to(block, out_ref.shape)


def last_kernel(
    in_ref, gain_ref, offset_ref, lw_ref, lb_ref, rw_ref, rb_ref, w_ref, wb_ref, w_scratch
):
    blocks = in_ref[...].astype(F32)
    w_scratch[...] = blocks[:, :WR].reshape(C * C, Z)
    for c in range(C):
        w_ref[c * C : (c + 1) * C, :] = w_scratch[pl.ds(c, C, stride=C), :]
    small = blocks[:, WR : WR + 16] + blocks[:, WR + 16 :]
    weights = small[:, :8].reshape(Z, Z)
    rest = small[0, 8:]
    lw_ref[:, :Z] = weights[:C]
    lw_ref[:, Z:] = weights[2 * C : 3 * C]
    rw_ref[:, :Z] = weights[C : 2 * C]
    rw_ref[:, Z:] = weights[3 * C :]
    gain_ref[:, :Z] = rest[0:1]
    gain_ref[:, Z:] = rest[1:2]
    offset_ref[:, :Z] = rest[2:3]
    offset_ref[:, Z:] = rest[3:4]
    lb_ref[...] = rest[4:5, :C]
    rb_ref[...] = rest[4:5, C : 2 * C]
    wb_ref[...] = rest[5:6] * ROOT


def shape(dims, dtype):
    return jax.ShapeDtypeStruct(dims, dtype)


LATE = pl.CostEstimate(flops=100_000_000_000, bytes_accessed=0, transcendentals=0)
HBM = pl.BlockSpec(memory_space=pltpu.HBM)
VMEM = pl.BlockSpec(memory_space=pltpu.VMEM)


def in_hbm(array):
    return pltpu.with_memory_space_constraint(array, pltpu.HBM)


def in_vmem(*arrays):
    return [pltpu.with_memory_space_constraint(v, pltpu.VMEM) for v in arrays]


def ring(step, long):
    def number(x, z, y, core):
        return ((x % NX * NZ + z) * NY + y % NY) * 2 + core

    pairs = []
    for x, z, y, core in itertools.product(range(NX), range(NZ), range(NY), range(2)):
        by_x = long == (core == 0)
        target = number(x + step * by_x, z, y + step * (not by_x), core)
        pairs.append((number(x, z, y, core), target))
    return pairs


def shifted(arrays, long):
    moved = {
        k: lax.ppermute(arrays[k], ("x", "z", "y", "dp"), ring(k, long)) for k in (1, 3, 2)
    }
    return [arrays[0], moved[1], moved[2], moved[3]]


def call(body, name, mib, out_shape, scratch=(), **more):
    params = pltpu.CompilerParams(vmem_limit_bytes=mib * MIB)
    return pl.pallas_call(
        body, out_shape=out_shape, scratch_shapes=list(scratch), compiler_params=params, name=name, **more
    )


def exchange(array, axes):
    return lax.all_to_all(array, axes, 0, 0, tiled=True)


def per_device(x, gain, shift, k1, b1, k2, b2, w, bias, g):
    gain, shift, b1, b2, bias = [v.reshape(1, -1) for v in (gain, shift, b1, b2, bias)]
    x, k1, k2 = x.reshape(S * I, H), k1.T, k2.T
    inputs = (x, gain, shift, k1, b1, k2, b2, w, g)
    made = (
        ((I * S, C), BF16),
        ((G, C * S), BF16),
        ((C, C * Z), BF16),
        ((C * S, I * Z), BF16),
        (g.shape, BF16),
    )
    left, copies, wd, t, ordered, p0, p1, p2, p3 = call(
        first_kernel,
        "first",
        24,
        tuple(pltpu.HBM(*v) for v in made) + (pltpu.VMEM((Q, C * S), BF16),) * NX,
        [pltpu.VMEM(v.shape, v.dtype) for v in inputs]
        + [pltpu.VMEM(*v) for v in made]
        + [pltpu.VMEM((C * C, Z), F32), pltpu.VMEM(g.shape, F32), pltpu.SemaphoreType.DMA((len(inputs),))]
        + [pltpu.SemaphoreType.DMA((len(made),))],
        in_specs=[HBM] * len(inputs),
        out_specs=[HBM] * len(made) + [VMEM] * NX,
    )(*[in_hbm(v) for v in inputs])
    quarter = ((Q, C * S), BF16)
    column = ((G, C * S), BF16)
    planes = shifted((p0, p1, p2, p3), True)
    near = exchange(copies, "z")
    lines = shifted([near] * NY, False)
    parts = call(
        fold_kernel, "fold", 8, (pltpu.VMEM(*column),) * NY, [pltpu.VMEM((Q, C * S), F32)]
    )(*in_vmem(*planes))
    sums = shifted(parts, False)
    r0 = call(arrange_kernel, "arrange", 8, pltpu.VMEM(*quarter), [pltpu.VMEM((Q, C * S), F32)])(
        *in_vmem(*lines, parts[0])
    )
    rights = in_vmem(*shifted([r0] * NX, True))
    own = call(add_kernel, "add", 8, shape((G, C * S), F32), cost_estimate=LATE)(*in_vmem(*sums))
    pieces = exchange(own, "z")
    rt_type = ((C * S + 16, HALF), BF16)
    half = call(
        early_kernel,
        "early",
        16,
        pltpu.VMEM((C * S + 16, I * Z), F32),
        [pltpu.VMEM((I, HALF, Z), BF16), pltpu.VMEM(*rt_type), pltpu.SemaphoreType.DMA((2,))],
        in_specs=[VMEM] * 2 + [HBM],
    )(*[rights[k] for k in EARLY], in_hbm(ordered))
    left_grad, w_part, bias_grad = call(
        second_kernel,
        "second",
        16,
        (shape((I * S, C), F32), pltpu.HBM((C, C, Z), BF16), shape((1, Z), F32)),
        [pltpu.VMEM((I, HALF, Z), BF16), pltpu.VMEM(wd.shape, BF16)]
        + [pltpu.VMEM(*rt_type), pltpu.VMEM((I * S, C * Z), BF16)]
        + [pltpu.SemaphoreType.DMA((2,)), pltpu.SemaphoreType.DMA],
        in_specs=[VMEM] * 3 + [HBM] * 2 + [VMEM],
        cost_estimate=LATE,
    )(*[rights[k] for k in LATER], *in_vmem(half), in_hbm(ordered), in_hbm(wd), left)
    align, pack = call(
        third_kernel,
        "third",
        12,
        (pltpu.HBM((S * I, H), F32), shape((NP, WR + 32, Z), BF16)),
        [pltpu.VMEM((C, C, Z), BF16), pltpu.VMEM((S * I, H), F32)]
        + [pltpu.SemaphoreType.DMA, pltpu.SemaphoreType.DMA],
        out_specs=[HBM, VMEM],
        in_specs=[VMEM, HBM] + [VMEM] * 7,
    )(left_grad, in_hbm(w_part), bias_grad, x, gain, shift, k1, k2, pieces)
    parts = exchange(pack, ("x", "y"))
    update = call(
        update_kernel,
        "update",
        20,
        pltpu.HBM((I, J, Z), BF16),
        [pltpu.VMEM(t.shape, BF16), pltpu.VMEM((I, J, Z), BF16), pltpu.VMEM((J, I * Z), F32)]
        + [pltpu.SemaphoreType.DMA, pltpu.SemaphoreType.DMA((NX,))],
        in_specs=[VMEM] * NX + [HBM] + [VMEM],
        out_specs=HBM,
    )(*rights, in_hbm(t), bias)
    plane = call(sum_kernel, "sum", 8, shape((NZ, WR + 32, Z), BF16))(parts)
    column = exchange(plane, "z")
    block = call(sum_kernel, "spread", 8, shape((NP, WR + 32, Z), BF16))(column)
    sums = exchange(block, ("x", "y"))
    gain_g, offset_g, lw, lb, rw, rb, w_g, wb = call(
        last_kernel,
        "last",
        8,
        (
            shape((1, H), F32),
            shape((1, H), F32),
            shape((C, H), F32),
            shape((1, C), F32),
            shape((C, H), F32),
            shape((1, C), F32),
            shape((C * C, Z), F32),
            shape((1, Z), F32),
        ),
        [pltpu.VMEM((C * C, Z), F32)],
    )(sums)
    return (
        update,
        align.reshape(S, I, H),
        gain_g.reshape(H),
        offset_g.reshape(H),
        lw.T,
        lb.reshape(C),
        rw.T,
        rb.reshape(C),
        w_g,
        wb.reshape(Z),
    )


def solution(mesh):
    grid = Mesh(mesh.devices.reshape(NX, NZ, NY, 2), ("x", "z", "y", "dp"))
    dap = ("x", "z", "y")
    in_specs = (P("dp", dap, None),) + (P(),) * 8 + (P(("dp",) + dap, None, None),)
    out_specs = (
        P(("dp",) + dap, None, None),
        P("dp", dap, None),
        P("dp"),
        P("dp"),
        P("dp", None),
        P("dp"),
        P("dp", None),
        P("dp"),
        P("dp", None),
        P("dp"),
    )
    return jax.shard_map(
        per_device, mesh=grid, in_specs=in_specs, out_specs=out_specs, check_vma=False
    )
```
